512 devices in a mesh: dp: 16 (over y_lo, x), ctx: 32 (over z, y_hi, core).
Axes of the slice: x: 4, y: 8 (y_hi: 2, y_lo: 4; y = y_hi * 4 + y_lo), z: 8, core: 2. Of those that a mesh axis runs over, the one named last changes fastest.
Arguments:
- tokens: bfloat16 [65536, 1024], P(('dp', 'ctx')), may hold values from -6 to 6
- grad_out: bfloat16 [65536, 1024], P(('dp', 'ctx')), may hold values from -6 to 6
- gates: bfloat16 [65536, 8], P(('dp', 'ctx')), may hold values from 0.049804688 to 0.5
- expert_ids: int32 [65536, 8], P(('dp', 'ctx')), may hold values from 0 to 63, all different within a row; in each aligned block of 128 rows (0 to 127, 128 to 255, ...) at most 18 rows name the same one
- w_up: bfloat16 [64, 1024, 384], P('ctx', 'dp'), may hold values from -0.1875 to 0.1875
- w_down: bfloat16 [64, 384, 1024], P('ctx', None, 'dp'), may hold values from -0.3125 to 0.3125
Outputs:
- grad_tokens: bfloat16 [65536, 1024], P(('dp', 'ctx'))
- grad_gates: bfloat16 [65536, 8], P(('dp', 'ctx'))
- grad_up: bfloat16 [64, 1024, 384], P('ctx', 'dp')
- grad_down: bfloat16 [64, 384, 1024], P('ctx', None, 'dp')
The draws below stay inside these ranges and needn't reach their ends.
Inputs may be any that keep to these rules, and one draw needn't show every extreme that they name: `expert_ids`: each row names 8 different experts. Among the 128 rows of one device no expert is named more than 18 times, and in every draw some expert is named exactly 18 times in some device's rows.
All inputs are finite; a program needn't handle non-finite values.
Results may differ from the reference program's by a relative error of at most 0.023.
Values may be sent and summed in bfloat16 or wider, within the bound.
No kernel may reach another device: no remote copies, remote signals or barrier semaphores. Data moves between devices by JAX's collectives and lax.ppermute only.
A program may use at most 64 MiB of HBM per device.

```python
import math
import jax
import jax.numpy as jnp
import numpy as np
from jax import lax

D = 1024
FF = 384
TOP = 8
TOK_DEV = 128
EXPERTS = 64
CAP = 18
TOKENS = 65536
N_DP = 16
N_CTX = 32


def shard_levels(stream_key, dims, shards, smallest, top_value):
    level = 1.0
    for dim, shards_of in shards:
        heights = jax.random.uniform(jax.random.fold_in(jax.random.fold_in(stream_key, 6), dim), (shards_of,), jnp.float32, smallest / len(shards), top_value / len(shards))
        level = level * jnp.repeat(jnp.exp(heights), dims[dim] // shards_of).reshape((-1,) + (1,) * (len(dims) - 1 - dim))
    return level


def shared_out(stream_key, own, number, rows, number_of, top, limit, slope):
    order = jax.random.permutation(stream_key, number_of)
    heavy_load, common = shares(number_of, rows * top, limit, slope, True), shares(number_of, rows * top, limit, slope, False)
    places = jnp.arange(number_of)

    def named(sizes, turn):
        used = int((sizes > 0).sum())
        fixed = max(1, used // 4)
        passed = fixed + (places - fixed + turn * (used - fixed)) % max(1, number_of - fixed)
        return jnp.zeros((number_of,), jnp.int32).at[order[jnp.where(places < fixed, places, passed)]].set(jnp.asarray(sizes, jnp.int32))

    sizes = jnp.where(number % 4 == 0, named(heavy_load, number // 4), named(common, number - number // 4 - 1))
    mixed = jax.random.permutation(jax.random.fold_in(own, 3), number_of)
    giver, taker = mixed[0:number_of // 2 * 2:2], mixed[1:number_of // 2 * 2:2]
    slack = jnp.minimum(sizes[giver] - 1, limit - sizes[taker]) // 2
    slack = jnp.where((giver == order[0]) | (taker == order[0]) | (sizes[taker] == 0), 0, jnp.maximum(slack, 0))
    passed = jax.random.randint(jax.random.fold_in(own, 4), (number_of // 2,), 0, 1 << 20) % (slack + 1)
    sizes = sizes.at[giver].add(-passed).at[taker].add(passed)
    members = jnp.searchsorted(jnp.cumsum(sizes), jnp.arange(rows * top), side="right").astype(jnp.int32)
    table = members.reshape(top, rows).T
    table = table[jax.random.permutation(jax.random.fold_in(own, 1), rows)]
    turn = jax.random.randint(jax.random.fold_in(own, 2), (rows, 1), 0, top)
    return jnp.take_along_axis(table, (jnp.arange(top)[None, :] + turn) % top, axis=1)


def shares(number_of, total, most, lean, full):
    loads = [(1 << 20) // math.isqrt(standing ** lean) + 1 for standing in range(1, number_of + 1)]
    largest = most if full else min(most, max(-(-total // number_of), total * loads[0] // sum(loads)))
    least = 1 if total - largest >= number_of - 1 else 0
    holding, rest = [largest] + [least] * (number_of - 1), total - largest - least * (number_of - 1)
    while rest > 0:
        free = [i for i in range(1, number_of) if holding[i] < largest] or [i for i in range(1, number_of) if holding[i] < most]
        mass, remaining = sum([loads[i] for i in free]), rest
        for i in free:
            extra = min(most - holding[i], max(1, remaining * loads[i] // mass), rest)
            holding[i] = holding[i] + extra
            rest = rest - extra
    return np.array(holding)


def bell_draw(stream_key, shape, scale, reach, pieces=(), kind=jnp.bfloat16):
    loudness = shard_levels(stream_key, shape, pieces, -0.22, 0.18) if pieces else 1.0
    values = jax.random.normal(stream_key, shape, jnp.float32) * scale * loudness
    return jnp.minimum(jnp.maximum(values, -reach), reach).astype(kind)


def setup_inputs(seed: int = 0) -> dict:
    seeds = jax.random.split(jax.random.key(seed), 7)
    tokens = bell_draw(seeds[0], (TOKENS, D), 1.0, 6.0, ((0, 512),))
    grad_out = bell_draw(seeds[1], (TOKENS, D), 1.0, 6.0, ((0, 512),))
    gates = jnp.clip(0.049804688 + 0.4501953 * jax.random.uniform(seeds[2], (TOKENS, TOP), jnp.float32) ** shard_levels(seeds[2], (TOKENS, TOP), ((0, 512),), -0.2, 0.2), 0.049804688, 0.5).astype(jnp.bfloat16)
    expert_ids_keys = jax.random.split(jax.random.fold_in(seeds[3], 1), TOKENS // TOK_DEV)
    expert_ids_turns = jax.random.permutation(jax.random.fold_in(seeds[3], 3), TOKENS // TOK_DEV)
    expert_ids = jax.vmap(lambda own, number: shared_out(jax.random.fold_in(seeds[3], 2), own, number, TOK_DEV, EXPERTS, TOP, CAP, 2))(expert_ids_keys, expert_ids_turns).reshape((TOKENS, TOP))
    w_up = bell_draw(seeds[4], (EXPERTS, D, FF), D ** -0.5, 0.1875, ((0, 32), (1, 16)))
    w_down = bell_draw(seeds[5], (EXPERTS, FF, D), FF ** -0.5, 0.3125, ((0, 32), (2, 16)))
    return {"tokens": tokens, "grad_out": grad_out, "gates": gates, "expert_ids": expert_ids, "w_up": w_up, "w_down": w_down}


def swish_grad(pre_act, sigmoid_a):
    return sigmoid_a * (1.0 + pre_act * (1.0 - sigmoid_a))

def reference(tokens, grad_out, gates, expert_ids, w_up, w_down):
    group_len = TOK_DEV * N_CTX
    row_cap = CAP * N_CTX
    choice_len = group_len * TOP

    def one_group(totals, group_idx):
        begin = (group_idx * group_len).astype(jnp.int32)
        group_x = lax.dynamic_slice_in_dim(tokens, begin, group_len, 0)
        group_grad = lax.dynamic_slice_in_dim(grad_out, begin, group_len, 0)
        flat_gates = lax.dynamic_slice_in_dim(gates, begin, group_len, 0).reshape(-1)
        flat_ids = lax.dynamic_slice_in_dim(expert_ids, begin, group_len, 0).reshape(-1)

        def one_expert(expert):
            keys = (flat_ids != expert).astype(jnp.int32)
            picked = jnp.argsort(keys, stable=True)[:row_cap].astype(jnp.int32)
            is_valid = flat_ids[picked] == expert
            token_pos = picked // TOP
            rows_x = jnp.where(is_valid[:, None], group_x[token_pos], jnp.zeros((), group_x.dtype))
            rows_grad = jnp.where(is_valid[:, None], group_grad[token_pos], jnp.zeros((), group_grad.dtype))
            rows_gate = jnp.where(is_valid, flat_gates[picked], jnp.zeros((), flat_gates.dtype))
            up_mat = w_up[expert]
            down_mat = w_down[expert]
            pre_act = jnp.dot(rows_x, up_mat, preferred_element_type=jnp.float32)
            sigmoid_a = jax.nn.sigmoid(pre_act)
            hidden = (pre_act * sigmoid_a).astype(jnp.bfloat16)
            outputs = jnp.dot(hidden, down_mat, preferred_element_type=jnp.float32).astype(jnp.bfloat16)
            grad_y = (rows_gate[:, None].astype(jnp.float32) * rows_grad.astype(jnp.float32)).astype(jnp.bfloat16)
            scores = lax.optimization_barrier(jnp.sum(rows_grad.astype(jnp.float32) * outputs.astype(jnp.float32), axis=1)).astype(jnp.bfloat16)
            grad_h = jnp.dot(grad_y, down_mat.T, preferred_element_type=jnp.float32)
            grad_a = (grad_h * swish_grad(pre_act, sigmoid_a)).astype(jnp.bfloat16)
            grad_rows = jnp.dot(grad_a, up_mat.T, preferred_element_type=jnp.float32).astype(jnp.bfloat16)
            part_up = jnp.dot(rows_x.T, grad_a, preferred_element_type=jnp.float32).astype(jnp.bfloat16)
            part_down = jnp.dot(hidden.T, grad_y, preferred_element_type=jnp.float32).astype(jnp.bfloat16)
            return (picked, grad_rows, scores, part_up, part_down)
        picked, grad_rows, scores, part_up, part_down = lax.map(one_expert, jnp.arange(EXPERTS, dtype=jnp.int32))
        flat_pick = picked.reshape(-1)
        row_sums = jnp.zeros((choice_len, D), jnp.float32).at[flat_pick].add(grad_rows.reshape(-1, D).astype(jnp.float32))
        score_sums = jnp.zeros((choice_len,), jnp.float32).at[flat_pick].add(scores.reshape(-1).astype(jnp.float32))
        group_tokens = lax.optimization_barrier(jnp.sum(row_sums.reshape(group_len, TOP, D), axis=1)).astype(jnp.bfloat16)
        group_gates = score_sums.reshape(group_len, TOP).astype(jnp.bfloat16)
        new_totals = (totals[0] + part_up.astype(jnp.float32), totals[1] + part_down.astype(jnp.float32))
        return (new_totals, (group_tokens, group_gates))
    start_totals = (jnp.zeros((EXPERTS, D, FF), jnp.float32), jnp.zeros((EXPERTS, FF, D), jnp.float32))
    totals, (all_tokens, all_gates) = lax.scan(one_group, start_totals, jnp.arange(N_DP, dtype=jnp.int32))
    grad_tokens = all_tokens.reshape(TOKENS, D)
    grad_gates = all_gates.reshape(TOKENS, TOP)
    return (grad_tokens, grad_gates, totals[0].astype(jnp.bfloat16), totals[1].astype(jnp.bfloat16))
```

```python
import functools

import jax
import jax.numpy as jnp
from jax import lax
from jax.experimental import pallas as pl
from jax.experimental.pallas import tpu as pltpu
from jax.sharding import Mesh, PartitionSpec as P

BF, F32 = jnp.bfloat16, jnp.float32
HALF = 64
SLOTS = 40


def params(mebibytes):
    return pltpu.CompilerParams(vmem_limit_bytes=mebibytes * 1024 * 1024)


def vmem(count):
    return [pl.BlockSpec(memory_space=pltpu.VMEM)] * count


def dot(a, b, ca=1, cb=0):
    return lax.dot_general(a, b, (((ca,), (cb,)), ((), ())), preferred_element_type=F32)


def iota(shape, dim):
    return lax.broadcasted_iota(jnp.int32, shape, dim)


def prepare_kernel(tok, gout, gates, ids, pay, table):
    rows, width = tok.shape
    lane = iota((rows, 128), 1)
    expert = jnp.where(lane < HALF, lane, lane - HALF)
    gate = gates[...].astype(F32)
    chosen = ids[...]
    gate_of = jnp.zeros((rows, 128), F32)
    named = jnp.zeros((rows, 128), F32)
    for k in range(ids.shape[1]):
        hit = chosen[:, k : k + 1] == expert
        gate_of = gate_of + jnp.where(hit, gate[:, k : k + 1], 0.0)
        named = named + jnp.where(hit, 1.0, 0.0)
    before = jnp.where(iota((rows, rows), 0) > iota((rows, rows), 1), 1.0, 0.0).astype(BF)
    place = named * (dot(before, named.astype(BF)) + 1.0)
    both = jnp.where(lane < HALF, gate_of, place)
    table[...] = both
    pay[:, :width] = tok[...]
    pay[:, width : 2 * width] = gout[...]
    pay[:, 2 * width :] = both.T.astype(BF)


def pick_kernel(cap, gath, sel, place, origin, own, sib):
    n_z, rows, lanes = gath.shape
    width = lanes - 128
    block = n_z * cap
    gates = gath[:, :HALF, width:].reshape(n_z * HALF, 128)
    places = gath[:, HALF:, width:].reshape(n_z * HALF, 128)
    for b in range(4):
        out = own if b < 2 else sib
        part = slice(b * block, (b + 1) * block)
        hit = dot(sel[part], places) == place[...]
        gate = jnp.sum(jnp.where(hit, dot(sel[part], gates), 0.0), axis=1, keepdims=True)
        ones = jnp.where(hit, 1.0, 0.0)
        pick = jnp.concatenate(
            [jnp.where(origin[...] == s, ones, 0.0).astype(BF) for s in range(n_z)], axis=1
        )
        step = min(width, 512)
        for c in range(0, width, step):
            data = gath[:, :, c : c + step].reshape(n_z * rows, step)
            out[b % 2, :, c : c + step] = dot(pick, data).astype(BF)
        out[b % 2, :, width:] = jnp.broadcast_to(gate, (block, 128)).astype(BF)


def expert_kernel(n_y, n_x, cap, spot, *refs):
    w_in = refs[:n_x]
    rows_in = refs[n_x : n_x + 4]
    perm_l, perm_r, perm_s, lane_of = refs[n_x + 4 : n_x + 8]
    g_out = refs[n_x + 8 : 2 * n_x + 8]
    back = refs[2 * n_x + 8]
    weights, parts, grads, marks = refs[2 * n_x + 9 :]
    at_y, at_x, at_b = spot[0], spot[1], spot[2]
    share = w_in[0].shape[2]
    width, hidden_len = weights.shape[1:]
    block = rows_in[0].shape[1]
    n_z = block // cap

    def spot_of(i, d):
        return lax.rem(at_y + i, n_y) * n_x + lax.rem(at_x + d, n_x)

    for i in range(n_y):
        for d in range(n_x):
            start = pl.multiple_of(spot_of(n_y - i, n_x - d) * share, share)
            for m in range(4):
                weights[m, pl.ds(start, share), :] = w_in[d][i, m]
    for e in range(2):
        up, down = weights[e], weights[2 + e]
        x = jnp.concatenate([r[e, :, :width] for r in rows_in], axis=0)
        g = jnp.concatenate([r[e, :, width : 2 * width] for r in rows_in], axis=0)
        gate = jnp.concatenate([r[e, :, 2 * width :] for r in rows_in], axis=0).astype(F32)[:, :1]
        pre = dot(x, up)
        q = dot(g, down)
        s = jax.nn.sigmoid(pre)
        hidden = pre * s
        score = jnp.sum(hidden.astype(BF).astype(F32) * q, axis=1, keepdims=True)
        grad_a = (gate * q * (s * (1.0 + pre * (1.0 - s)))).astype(BF)
        parts[:, e] = dot(x, grad_a, 0, 0).astype(BF).reshape(n_y * n_x, share, hidden_len)
        parts[:, 2 + e] = dot(g, (gate * hidden).astype(BF), 0, 0).astype(BF).reshape(
            n_y * n_x, share, hidden_len
        )
        rows = dot(grad_a, up, 1, 1).astype(BF)
        for b in range(4):
            part = slice(b * block, (b + 1) * block)
            to = slice(e * block, (e + 1) * block)
            grads[b, to] = rows[part]
            marks[b, to] = (score[part] * lane_of[to]).astype(BF)
    for d in range(n_x):
        for i in range(n_y):
            g_out[d][i] = parts[spot_of(i, d)]
    half = width // 2
    for b in range(4):
        left = dot(perm_l[...], grads[b, :, :half]) + dot(perm_r[...], grads[b, :, half:])
        first = left[:, :128] + dot(perm_s[...], marks[b])
        at = lax.bitwise_xor(at_b, b)
        back[:, at, :, :128] = first.astype(BF).reshape(n_z, 2 * SLOTS, 128)
        back[:, at, :, 128:] = left[:, 128:].astype(BF).reshape(n_z, 2 * SLOTS, half - 128)


def combine_kernel(cap, got, table, ids, sel, place_l, place_r, grad_tok, grad_gate):
    n_dev, _, half = got.shape
    rows = table.shape[0]
    places = table[...].astype(BF)
    at = dot(places, sel[...])
    data = got[...].reshape(n_dev * 2 * SLOTS, half)
    grad_tok[:, :half] = dot((at == place_l[...]).astype(F32).astype(BF), data).astype(BF)
    grad_tok[:, half:] = dot((at == place_r[...]).astype(F32).astype(BF), data).astype(BF)
    scores = got[:, 32:48, :128].reshape(n_dev * 16, 128)
    lane = iota((rows, 128), 1)
    column = iota((rows, n_dev * 16), 1)
    column_out = iota((rows, ids.shape[1]), 1)
    chosen = ids[...]
    total = jnp.zeros((rows, ids.shape[1]), F32)
    for k in range(ids.shape[1]):
        e = chosen[:, k : k + 1]
        rank = jnp.sum(jnp.where(lane == e + HALF, table[...], 0.0), axis=1, keepdims=True) - 1.0
        owner = lax.shift_right_logical(e, 1)
        slot = rank.astype(jnp.int32) + (e & 1) * cap
        line = dot(jnp.where(column == owner * 16 + 4, 1.0, 0.0).astype(BF), scores)
        score = jnp.sum(jnp.where(lane == slot, line, 0.0), axis=1, keepdims=True)
        total = total + jnp.where(column_out == k, score, 0.0)
    grad_gate[...] = total.astype(BF)


def shift(value, axis, by):
    n = lax.axis_size(axis)
    return lax.ppermute(value, axis, [(i, (i + by) % n) for i in range(n)])


def per_device(tokens, grad_out, gates, expert_ids, w_up, w_down):
    rows, width = tokens.shape
    top = expert_ids.shape[1]
    n_y, n_x, n_z = lax.axis_size("yl"), lax.axis_size("x"), lax.axis_size("z")
    n_dev = 4 * n_z
    experts = 2 * n_dev
    cap = rows * top * 9 // (8 * experts)
    block = n_z * cap
    share, hidden_len = w_up.shape[1:]
    half = width // 2
    yl, x, z, yh, c = [lax.axis_index(a) for a in ("yl", "x", "z", "yh", "c")]
    shape = jax.ShapeDtypeStruct

    pay, table = pl.pallas_call(
        prepare_kernel,
        out_shape=(shape((rows, 2 * width + 128), BF), shape((rows, 128), F32)),
        in_specs=vmem(4),
        out_specs=tuple(vmem(2)),
        compiler_params=params(8),
    )(tokens, grad_out, gates, expert_ids)
    pay_other = shift(pay, "yh", 1)
    w_mine = jnp.concatenate((w_up, jnp.transpose(w_down, (0, 2, 1))), axis=0)
    w_line = jnp.stack([w_mine] + [shift(w_mine, "yl", d) for d in range(1, n_y)])
    gath_own = lax.all_gather(pay, "z", axis=0)
    gath_other = lax.all_gather(pay_other, "z", axis=0)
    gath_own, w_line = lax.optimization_barrier((gath_own, w_line))
    w_all = [w_line] + [shift(w_line, "x", d) for d in range(1, n_x)]
    gath_other, *w_all = lax.optimization_barrier((gath_other, *w_all))

    j = jnp.arange(4 * block)
    b_j, z_j, r_j = j // block, (j % block) // cap, j % cap
    core_j = jnp.where(b_j >= 2, 1 - c, c)
    e_j = ((z * 2 + yh) * 2 + core_j) * 2 + b_j % 2
    sel = ((z_j * HALF + e_j)[:, None] == jnp.arange(n_z * HALF)[None, :]).astype(BF)
    place = jnp.broadcast_to((r_j[:block, None] + 1).astype(F32), (block, 128))
    origin = jnp.broadcast_to(z_j[:block, None].astype(jnp.int32), (block, 128))

    def picked(gath):
        return pl.pallas_call(
            functools.partial(pick_kernel, cap),
            out_shape=(shape((2, block, 2 * width + 128), BF),) * 2,
            in_specs=vmem(4),
            out_specs=tuple(vmem(2)),
            compiler_params=params(20),
        )(gath, sel, place, origin)

    a_own, a_sib = picked(gath_own)
    a_got = shift(a_sib, "c", 1)
    b_own, b_sib = picked(gath_other)
    b_got = shift(b_sib, "c", 1)

    i = jnp.arange(2 * block)
    e_i, z_i, r_i = i // block, (i % block) // cap, i % cap
    p = jnp.arange(n_z * 2 * SLOTS)
    z_p, q_p = p // (2 * SLOTS), p % (2 * SLOTS)
    same = z_p[:, None] == z_i[None, :]
    slot_i = (e_i * cap + r_i)[None, :]
    perm_l = (same & (q_p[:, None] == slot_i)).astype(BF)
    perm_r = (same & (q_p[:, None] == slot_i + SLOTS)).astype(BF)
    perm_s = (same & (q_p[:, None] == 2 * cap)).astype(BF)
    lane_of = (slot_i.T == jnp.arange(128)[None, :]).astype(F32)
    spot = jnp.stack([yl, x, yh * 2 + c]).astype(jnp.int32)
    outs = pl.pallas_call(
        functools.partial(expert_kernel, n_y, n_x, cap),
        out_shape=(shape((n_y, 4, share, hidden_len), BF),) * n_x
        + (shape((n_z, 4, 2 * SLOTS, half), BF),),
        in_specs=[pl.BlockSpec(memory_space=pltpu.SMEM)] + vmem(n_x + 8),
        out_specs=tuple(vmem(n_x + 1)),
        scratch_shapes=[
            pltpu.VMEM((4, width, hidden_len), BF),
            pltpu.VMEM((n_y * n_x, 4, share, hidden_len), BF),
            pltpu.VMEM((4, 2 * block, width), BF),
            pltpu.VMEM((4, 2 * block, 128), BF),
        ],
        compiler_params=params(36),
    )(spot, *w_all, a_own, a_got, b_own, b_got, perm_l, perm_r, perm_s, lane_of)
    parts, back = outs[:n_x], outs[n_x]
    got = lax.all_to_all(
        back.reshape(n_dev, 2 * SLOTS, half), ("z", "yh", "c"), 0, 0, tiled=True
    )

    lines = [parts[0]] + [shift(parts[d], "x", d) for d in range(1, n_x)]
    line = sum(v.astype(F32) for v in lines).astype(BF)
    ends = [line[0]] + [shift(line[d], "yl", d) for d in range(1, n_y)]
    summed = sum(v.astype(F32) for v in ends).astype(BF)
    grad_up = summed[:2]
    grad_down = jnp.transpose(summed[2:], (0, 2, 1))

    dev_p, s_p = jnp.arange(n_dev * 2 * SLOTS) // (2 * SLOTS), jnp.arange(n_dev * 2 * SLOTS) % (2 * SLOTS)
    q = s_p % SLOTS
    sel_c = (jnp.arange(128)[:, None] == (HALF + dev_p * 2 + (q >= cap))[None, :]).astype(BF)
    tgt = jnp.where(q < 2 * cap, q % cap + 1, -1)
    place_l = jnp.where(s_p < SLOTS, tgt, -1).astype(F32)[None, :]
    place_r = jnp.where(s_p >= SLOTS, tgt, -1).astype(F32)[None, :]
    grad_tokens, grad_gates = pl.pallas_call(
        functools.partial(combine_kernel, cap),
        out_shape=(shape((rows, width), BF), shape((rows, top), BF)),
        in_specs=vmem(6),
        out_specs=tuple(vmem(2)),
        compiler_params=params(14),
    )(got, table, expert_ids, sel_c, place_l, place_r)
    return (grad_tokens, grad_gates, grad_up, grad_down)


def build(mesh):
    every, dp, ctx = ("yl", "x", "z", "yh", "c"), ("yl", "x"), ("z", "yh", "c")
    tok, up, down = P(every, None), P(ctx, dp, None), P(ctx, None, dp)
    return jax.shard_map(
        per_device,
        mesh=mesh,
        in_specs=(tok, tok, tok, tok, up, down),
        out_specs=(tok, tok, up, down),
        check_vma=False,
    )


def solution(mesh):
    return build(Mesh(mesh.devices.reshape(4, 4, 8, 2, 2), ("yl", "x", "z", "yh", "c")))
```

```python
import functools

import jax
import jax.numpy as jnp
from jax import lax
from jax.experimental import pallas as pl
from jax.experimental.pallas import tpu as pltpu
from jax.sharding import Mesh, PartitionSpec as P

BF, F32 = jnp.bfloat16, jnp.float32
HALF = 64
SLOTS = 40


def params(mebibytes):
    return pltpu.CompilerParams(vmem_limit_bytes=mebibytes * 1024 * 1024)


def cost(gflop, mebibytes):
    return pl.CostEstimate(
        flops=int(gflop * 1e9), bytes_accessed=int(mebibytes * 2**20), transcendentals=0
    )


def vmem(count):
    return [pl.BlockSpec(memory_space=pltpu.VMEM)] * count


def dot(a, b, ca=1, cb=0):
    return lax.dot_general(a, b, (((ca,), (cb,)), ((), ())), preferred_element_type=F32)


def iota(shape, dim):
    return lax.broadcasted_iota(jnp.int32, shape, dim)


def prepare_kernel(tok, gout, gates, ids, pay, table):
    rows, width = tok.shape
    lane = iota((rows, 128), 1)
    expert = jnp.where(lane < HALF, lane, lane - HALF)
    gate = gates[...].astype(F32)
    chosen = ids[...]
    gate_of = jnp.zeros((rows, 128), F32)
    named = jnp.zeros((rows, 128), F32)
    for k in range(ids.shape[1]):
        hit = chosen[:, k : k + 1] == expert
        gate_of = gate_of + jnp.where(hit, gate[:, k : k + 1], 0.0)
        named = named + jnp.where(hit, 1.0, 0.0)
    before = jnp.where(iota((rows, rows), 0) > iota((rows, rows), 1), 1.0, 0.0).astype(BF)
    place = named * (dot(before, named.astype(BF)) + 1.0)
    both = jnp.where(lane < HALF, gate_of, place)
    table[...] = both
    pay[:, :width] = tok[...]
    pay[:, width : 2 * width] = gout[...]
    pay[:, 2 * width :] = both.T.astype(BF)


def pick_kernel(cap, n_z, *refs):
    blocks = refs[: n_z + 1]
    sel, place, origin = refs[n_z + 1 : n_z + 4]
    own, sib = refs[-2:]
    rows, lanes = blocks[0].shape
    width = lanes - 128
    mid = n_z // 2
    block = n_z * cap
    tops = [b for i, b in enumerate(blocks) if i != mid + 1]
    ends = [b for i, b in enumerate(blocks) if i != mid]
    gates = jnp.concatenate([b[:HALF, width:] for b in tops], axis=0)
    places = jnp.concatenate(
        [b[b.shape[0] - HALF :, width:] for b in ends], axis=0
    )
    hits, gate_cols = [], []
    for b in range(4):
        part = slice(b * block, (b + 1) * block)
        hit = dot(sel[part], places) == place[...]
        gate_cols.append(
            jnp.sum(jnp.where(hit, dot(sel[part], gates), 0.0), axis=1, keepdims=True)
        )
        ones = jnp.where(hit, 1.0, 0.0)
        hits.append(
            jnp.concatenate(
                [jnp.where(origin[...] == s, ones, 0.0).astype(BF) for s in range(n_z)], axis=1
            )
        )
    step = min(width, 512)
    for b in range(4):
        out = own if b < 2 else sib
        for c in range(0, width, step):
            data = jnp.concatenate([r[:, c : c + step] for r in blocks], axis=0)
            out[b % 2, :, c : c + step] = dot(hits[b], data).astype(BF)
        out[b % 2, :, width:] = jnp.broadcast_to(gate_cols[b], (block, 128)).astype(BF)


def expert_kernel(cap, spot, w_ref, own, got, perm_l, perm_r, perm_s, lane_of, back, fac_up, fac_down, grads, marks):
    rows_in = (own, got)
    width = w_ref.shape[1]
    block = own.shape[1]
    n_z = block // cap
    half = width // 2
    for e in range(2):
        up, down = w_ref[e], w_ref[2 + e]
        x = jnp.concatenate([r[e, :, :width] for r in rows_in], axis=0)
        g = jnp.concatenate([r[e, :, width : 2 * width] for r in rows_in], axis=0)
        gate = jnp.concatenate([r[e, :, 2 * width :] for r in rows_in], axis=0).astype(F32)[:, :1]
        pre = dot(x, up)
        q = dot(g, down)
        s = jax.nn.sigmoid(pre)
        hidden = pre * s
        score = jnp.sum(hidden.astype(BF).astype(F32) * q, axis=1, keepdims=True)
        grad_a = (gate * q * (s * (1.0 + pre * (1.0 - s)))).astype(BF)
        fac_up[e] = grad_a
        fac_down[e] = (gate * hidden).astype(BF)
        rows = dot(grad_a, up, 1, 1).astype(BF)
        for b in range(2):
            part = slice(b * block, (b + 1) * block)
            to = slice(e * block, (e + 1) * block)
            grads[b, to] = rows[part]
            marks[b, to] = (score[part] * lane_of[to]).astype(BF)
    for b in range(2):
        left = dot(perm_l[...], grads[b, :, :half]) + dot(perm_r[...], grads[b, :, half:])
        first = left[:, :128] + dot(perm_s[...], marks[b])
        at = lax.bitwise_xor(spot[2], b)
        back[:, at, :, :128] = first.astype(BF).reshape(n_z, 2 * SLOTS, 128)
        back[:, at, :, 128:] = left[:, 128:].astype(BF).reshape(n_z, 2 * SLOTS, half - 128)


def weight_kernel(n_y, n_x, spot, *refs):
    rows_in, fac = refs[:4], refs[4:8]
    g_out, parts = refs[8 : 8 + n_x], refs[8 + n_x]
    share, hidden_len = parts.shape[2:]
    width = parts.shape[0] * share
    for e in range(2):
        for m in range(2):
            x = jnp.concatenate([r[e, :, m * width : (m + 1) * width] for r in rows_in], axis=0)
            f = jnp.concatenate((fac[m][e], fac[2 + m][e]), axis=0)
            parts[:, 2 * m + e] = dot(x, f, 0, 0).astype(BF).reshape(-1, share, hidden_len)
    for d in range(n_x):
        for i in range(n_y):
            g_out[d][i] = parts[lax.rem(spot[0] + i, n_y) * n_x + lax.rem(spot[1] + d, n_x)]


def total_kernel(*refs):
    *ends, up, down = refs
    up[...] = sum(r[:2].astype(F32) for r in ends).astype(BF)
    down[...] = sum(r[2:].astype(F32) for r in ends).astype(BF)


def partial_sums(cap, got, at, lane_places, owners, slots, place_l, place_r):
    n_dev, _, half = got.shape
    data = got[...].reshape(n_dev * 2 * SLOTS, half)
    left = dot((at == place_l[...]).astype(F32).astype(BF), data)
    right = dot((at == place_r[...]).astype(F32).astype(BF), data)
    lines = got[:, 32:48, :128].reshape(n_dev * 16, 128)
    by_place = jnp.zeros((slots.shape[1], 128), F32)
    for m in range(2):
        by_place = by_place + dot(dot(slots[m], lines, 1, 1).astype(BF), owners[m])
    scores = jnp.zeros(lane_places.shape, F32)
    for r in range(cap):
        scores = scores + jnp.where(lane_places == r + 1.0, by_place[r : r + 1, :], 0.0)
    return left, right, scores


def partner_kernel(cap, got, pay, sel, owners, slots, place_l, place_r, out):
    width = out.shape[1] - 128
    half = width // 2
    meta = pay[HALF:, 2 * width :]
    at = dot(meta, sel[...], 0, 0)
    lane = iota((HALF, 128), 0) == iota((HALF, 128), 1)
    lane_places = dot(meta, jnp.where(lane, 1.0, 0.0).astype(BF), 0, 0)
    left, right, scores = partial_sums(cap, got, at, lane_places, owners, slots, place_l, place_r)
    out[:, :half] = left.astype(BF)
    out[:, half:width] = right.astype(BF)
    out[:, width:] = scores.astype(BF)


def combine_kernel(cap, got, table, ids, sel, owners, slots, place_l, place_r, other, grad_tok, grad_gate):
    rows, width = grad_tok.shape
    half = width // 2
    both = table[...]
    at = dot(both.astype(BF), sel[...])
    at_lane = iota((128, 128), 0) == iota((128, 128), 1) + HALF
    lane_places = dot(both.astype(BF), jnp.where(at_lane, 1.0, 0.0).astype(BF))
    left, right, scores = partial_sums(cap, got, at, lane_places, owners, slots, place_l, place_r)
    grad_tok[:, :half] = (left + other[:, :half].astype(F32)).astype(BF)
    grad_tok[:, half:] = (right + other[:, half:width].astype(F32)).astype(BF)
    scores = scores + other[:, width:].astype(F32)
    lane = iota((rows, 128), 1)
    column = iota((rows, ids.shape[1]), 1)
    chosen = ids[...]
    total = jnp.zeros((rows, ids.shape[1]), F32)
    for k in range(ids.shape[1]):
        score = jnp.sum(
            jnp.where(lane == chosen[:, k : k + 1], scores, 0.0), axis=1, keepdims=True
        )
        total = total + jnp.where(column == k, score, 0.0)
    grad_gate[...] = total.astype(BF)


def shift(value, axis, by):
    n = lax.axis_size(axis)
    return lax.ppermute(value, axis, [(i, (i + by) % n) for i in range(n)])


def together(values, after=()):
    anywhere = pl.BlockSpec(memory_space=pl.ANY)
    return pl.pallas_call(
        lambda *refs: None,
        out_shape=tuple(jax.ShapeDtypeStruct(v.shape, v.dtype) for v in values),
        in_specs=[anywhere] * (len(values) + len(after)),
        out_specs=(anywhere,) * len(values),
        input_output_aliases={i: i for i in range(len(values))},
    )(*values, *after)


def rings(block):
    steps = lax.axis_size("z") // 2
    rows = block.shape[0] // 2
    chains = [([block], [block]), ([], [])]

    def advance(chain):
        below, above = chain
        if len(below) < steps:
            below.append(shift(below[-1], "z", 1))
            above.append(shift(above[-1], "z", -1))
        elif len(below) == steps:
            below.append(shift(below[-1][:rows], "z", 1))
            above.append(shift(above[-1][rows:], "z", -1))

    def settle():
        ends = [chain[-1] for pair in chains for chain in pair]
        ends[2:] = ends[2:] if ends[2] is not ends[3] else ends[2:3]
        held = together(ends)
        for n, chain in enumerate(chain for pair in chains for chain in pair):
            chain[-1] = held[min(n, len(held) - 1)]

    partner = shift(block, "yh", 1)
    advance(chains[0])
    advance(chains[0])
    for chain in chains[1]:
        chain.append(partner)
    settle()
    partner = chains[1][0][0]
    while len(chains[0][0]) <= steps:
        advance(chains[0])
        advance(chains[1])
        settle()
    while len(chains[1][0]) <= steps:
        advance(chains[1])
    order = [
        below[:steps] + [below[steps], above[steps]] + above[steps - 1 : 0 : -1]
        for below, above in chains
    ]
    return partner, order[0], order[1]


def per_device(tokens, grad_out, gates, expert_ids, w_up, w_down):
    rows, width = tokens.shape
    top = expert_ids.shape[1]
    n_y, n_x, n_z = lax.axis_size("yl"), lax.axis_size("x"), lax.axis_size("z")
    experts = 8 * n_z
    cap = rows * top * 9 // (8 * experts)
    block = n_z * cap
    share, hidden_len = w_up.shape[1:]
    half = width // 2
    yl, x, z, yh, c = [lax.axis_index(a) for a in ("yl", "x", "z", "yh", "c")]
    shape = jax.ShapeDtypeStruct

    pay, table = pl.pallas_call(
        prepare_kernel,
        out_shape=(shape((rows, 2 * width + 128), BF), shape((rows, 128), F32)),
        in_specs=vmem(4),
        out_specs=tuple(vmem(2)),
        cost_estimate=cost(0.1, 2),
        compiler_params=params(8),
    )(tokens, grad_out, gates, expert_ids)
    pay_other, blocks_own, blocks_other = rings(pay)
    w_mine = jnp.concatenate((w_up, jnp.transpose(w_down, (0, 2, 1))), axis=0)
    w_all = lax.all_gather(w_mine, ("yl", "x"), axis=0)
    w_all = jnp.transpose(w_all, (1, 0, 2, 3)).reshape(4, width, hidden_len)

    j = jnp.arange(4 * block)
    b_j, d_j, r_j = j // block, (j % block) // cap, j % cap
    core_j = jnp.where(b_j >= 2, 1 - c, c)
    e_j = ((z * 2 + yh) * 2 + core_j) * 2 + b_j % 2
    sel = ((d_j * HALF + e_j)[:, None] == jnp.arange(n_z * HALF)[None, :]).astype(BF)
    place = jnp.broadcast_to((r_j[:block, None] + 1).astype(F32), (block, 128))
    origin = jnp.broadcast_to(d_j[:block, None].astype(jnp.int32), (block, 128))

    def picked(blocks, after=()):
        own, sib = pl.pallas_call(
            functools.partial(pick_kernel, cap, n_z),
            out_shape=(shape((2, block, 2 * width + 128), BF),) * 2,
            in_specs=vmem(n_z + 4) + [pl.BlockSpec(memory_space=pl.ANY)] * len(after),
            out_specs=tuple(vmem(2)),
            cost_estimate=cost(2.6, 12),
        compiler_params=params(20),
        )(*blocks, sel, place, origin, *after)
        return own, shift(sib, "c", 1)

    i = jnp.arange(2 * block)
    e_i, d_i, r_i = i // block, (i % block) // cap, i % cap
    z_i = (z + n_z - d_i) % n_z
    p = jnp.arange(n_z * 2 * SLOTS)
    z_p, q_p = p // (2 * SLOTS), p % (2 * SLOTS)
    same = z_p[:, None] == z_i[None, :]
    slot_i = (e_i * cap + r_i)[None, :]
    perm_l = (same & (q_p[:, None] == slot_i)).astype(BF)
    perm_r = (same & (q_p[:, None] == slot_i + SLOTS)).astype(BF)
    perm_s = (same & (q_p[:, None] == 2 * cap)).astype(BF)
    lane_of = (slot_i.T == jnp.arange(128)[None, :]).astype(F32)
    spot = jnp.stack([yl, x, c]).astype(jnp.int32)

    def worked(own, got):
        return pl.pallas_call(
            functools.partial(expert_kernel, cap),
            out_shape=(shape((n_z, 2, 2 * SLOTS, half), BF),)
            + (shape((2, 2 * block, hidden_len), BF),) * 2,
            in_specs=[pl.BlockSpec(memory_space=pltpu.SMEM)] + vmem(7),
            out_specs=tuple(vmem(3)),
            scratch_shapes=[
                pltpu.VMEM((2, 2 * block, width), BF),
                pltpu.VMEM((2, 2 * block, 128), BF),
            ],
            cost_estimate=cost(4, 24),
        compiler_params=params(28),
        )(spot, w_all, own, got, perm_l, perm_r, perm_s, lane_of)

    def replies(back):
        return lax.all_to_all(
            back.reshape(2 * n_z, 2 * SLOTS, half), ("z", "c"), 0, 0, tiled=True
        )

    a_own, a_got = picked(blocks_own)
    a_back, a_up, a_down = worked(a_own, a_got)
    (a_back,) = together((a_back,), (blocks_other[n_z // 2 - 1], blocks_other[n_z // 2 + 2]))
    got_own = replies(a_back)
    b_own, b_got = picked(blocks_other, (a_up,))
    b_back, b_up, b_down = worked(b_own, b_got)
    parts = pl.pallas_call(
        functools.partial(weight_kernel, n_y, n_x),
        out_shape=(shape((n_y, 4, share, hidden_len), BF),) * n_x,
        in_specs=[pl.BlockSpec(memory_space=pltpu.SMEM)] + vmem(8),
        out_specs=tuple(vmem(n_x)),
        scratch_shapes=[pltpu.VMEM((n_y * n_x, 4, share, hidden_len), BF)],
        cost_estimate=cost(2, 18),
        compiler_params=params(28),
    )(spot, a_own, a_got, b_own, b_got, a_up, a_down, b_up, b_down)
    (b_back,) = together((b_back,), (got_own, parts[0]))
    got_other = replies(b_back)

    lines = [parts[0]] + [shift(parts[d], "x", d) for d in range(1, n_x)]
    line = sum(v.astype(F32) for v in lines).astype(BF)
    ends = [line[0]] + [shift(line[d], "yl", d) for d in range(1, n_y)]
    grad_up, grad_down = pl.pallas_call(
        total_kernel,
        out_shape=(shape((2, share, hidden_len), BF),) * 2,
        in_specs=vmem(n_y),
        out_specs=tuple(vmem(2)),
        cost_estimate=cost(0, 60),
        compiler_params=params(6),
    )(*ends)
    grad_down = jnp.transpose(grad_down, (0, 2, 1))

    n_dev = 2 * n_z
    p = jnp.arange(n_dev * 2 * SLOTS)
    dev_p, s_p = p // (2 * SLOTS), p % (2 * SLOTS)
    q = s_p % SLOTS
    first_of = ((dev_p // 2 * 2 + yh) * 2 + dev_p % 2) * 2
    e_p = (first_of + (q >= cap))[None, :]
    sel_t = (jnp.arange(128)[:, None] == HALF + e_p).astype(BF)
    sel_p = (jnp.arange(HALF)[:, None] == e_p).astype(BF)
    tgt = jnp.where(q < 2 * cap, q % cap + 1, -1)
    place_l = jnp.where(s_p < SLOTS, tgt, -1).astype(F32)[None, :]
    place_r = jnp.where(s_p >= SLOTS, tgt, -1).astype(F32)[None, :]
    line_o = jnp.arange(n_dev * 16)
    first_o = ((line_o // 32 * 2 + yh) * 2 + line_o // 16 % 2) * 2
    first_o = jnp.where(line_o % 16 == 2 * cap - 32, first_o, -2)
    parity = jnp.arange(2)[:, None, None]
    owners = (first_o[None, :, None] + parity == jnp.arange(128)[None, None, :]).astype(BF)
    at_slot = jnp.arange(24)[None, :, None]
    slots = (
        (at_slot < cap) & (jnp.arange(128)[None, None, :] == at_slot + parity * cap)
    ).astype(BF)
    partner = pl.pallas_call(
        functools.partial(partner_kernel, cap),
        out_shape=shape((rows, width + 128), BF),
        in_specs=vmem(7),
        out_specs=vmem(1)[0],
        cost_estimate=cost(0.4, 4),
        compiler_params=params(12),
    )(got_other, pay_other, sel_p, owners, slots, place_l, place_r)
    other = shift(partner, "yh", 1)
    grad_tokens, grad_gates = pl.pallas_call(
        functools.partial(combine_kernel, cap),
        out_shape=(shape((rows, width), BF), shape((rows, top), BF)),
        in_specs=vmem(9),
        out_specs=tuple(vmem(2)),
        cost_estimate=cost(0.4, 4),
        compiler_params=params(12),
    )(got_own, table, expert_ids, sel_t, owners, slots, place_l, place_r, other)
    return (grad_tokens, grad_gates, grad_up, grad_down)


def build(mesh):
    every, dp, ctx = ("yl", "x", "z", "yh", "c"), ("yl", "x"), ("z", "yh", "c")
    tok, up, down = P(every, None), P(ctx, dp, None), P(ctx, None, dp)
    return jax.shard_map(
        per_device,
        mesh=mesh,
        in_specs=(tok, tok, tok, tok, up, down),
        out_specs=(tok, tok, up, down),
        check_vma=False,
    )


def solution(mesh):
    return build(Mesh(mesh.devices.reshape(4, 4, 8, 2, 2), ("yl", "x", "z", "yh", "c")))
```

```python
import functools

import jax
import jax.numpy as jnp
from jax import lax
from jax.experimental import pallas as pl
from jax.experimental.pallas import tpu as pltpu
from jax.sharding import Mesh, PartitionSpec as P

BF, F32 = jnp.bfloat16, jnp.float32
HALF = 64
SLOTS = 40


def params(mebibytes):
    return pltpu.CompilerParams(vmem_limit_bytes=mebibytes * 1024 * 1024)


def cost(gflop, mebibytes):
    return pl.CostEstimate(
        flops=int(gflop * 1e9), bytes_accessed=int(mebibytes * 2**20), transcendentals=0
    )


def vmem(count):
    return [pl.BlockSpec(memory_space=pltpu.VMEM)] * count


def dot(a, b, ca=1, cb=0):
    return lax.dot_general(a, b, (((ca,), (cb,)), ((), ())), preferred_element_type=F32)


def iota(shape, dim):
    return lax.broadcasted_iota(jnp.int32, shape, dim)


def prepare_kernel(tok, gout, gates, ids, pay, table):
    rows, width = tok.shape
    lane = iota((rows, 128), 1)
    expert = jnp.where(lane < HALF, lane, lane - HALF)
    gate = gates[...].astype(F32)
    chosen = ids[...]
    gate_of = jnp.zeros((rows, 128), F32)
    named = jnp.zeros((rows, 128), F32)
    for k in range(ids.shape[1]):
        hit = chosen[:, k : k + 1] == expert
        gate_of = gate_of + jnp.where(hit, gate[:, k : k + 1], 0.0)
        named = named + jnp.where(hit, 1.0, 0.0)
    before = jnp.where(iota((rows, rows), 0) > iota((rows, rows), 1), 1.0, 0.0).astype(BF)
    place = named * (dot(before, named.astype(BF)) + 1.0)
    both = jnp.where(lane < HALF, gate_of, place)
    table[...] = both
    pay[:, :width] = tok[...]
    pay[:, width : 2 * width] = gout[...]
    pay[:, 2 * width :] = both.T.astype(BF)


def pick_kernel(cap, n_z, *refs):
    *blocks, sel, place, origin, own, sib = refs
    if len(blocks) == 1:
        blocks = tops = ends = [blocks[0].at[i] for i in range(n_z)]
    else:
        mid = n_z // 2
        tops = [b for i, b in enumerate(blocks) if i != mid + 1]
        ends = [b for i, b in enumerate(blocks) if i != mid]
    width = own.shape[2] - 128
    block = n_z * cap
    gates = jnp.concatenate([b[:HALF, width:] for b in tops], axis=0)
    places = jnp.concatenate(
        [b[b.shape[0] - HALF :, width:] for b in ends], axis=0
    )
    hits, gate_cols = [], []
    for b in range(4):
        part = slice(b * block, (b + 1) * block)
        hit = dot(sel[part], places) == place[...]
        gate_cols.append(
            jnp.sum(jnp.where(hit, dot(sel[part], gates), 0.0), axis=1, keepdims=True)
        )
        ones = jnp.where(hit, 1.0, 0.0)
        hits.append(
            jnp.concatenate(
                [jnp.where(origin[...] == s, ones, 0.0).astype(BF) for s in range(n_z)], axis=1
            )
        )
    step = min(width, 512)
    for b in range(4):
        out = own if b < 2 else sib
        for c in range(0, width, step):
            data = jnp.concatenate([r[:, c : c + step] for r in blocks], axis=0)
            out[b % 2, :, c : c + step] = dot(hits[b], data).astype(BF)
        out[b % 2, :, width:] = jnp.broadcast_to(gate_cols[b], (block, 128)).astype(BF)


def expert_kernel(cap, spot, w_ref, own, got, perm_l, perm_r, perm_s, lane_of, back, fac_up, fac_down, grads, marks):
    rows_in = (own, got)
    width = w_ref.shape[1]
    block = own.shape[1]
    n_z = block // cap
    half = width // 2
    for e in range(2):
        up, down = w_ref[e], w_ref[2 + e]
        x = jnp.concatenate([r[e, :, :width] for r in rows_in], axis=0)
        g = jnp.concatenate([r[e, :, width : 2 * width] for r in rows_in], axis=0)
        gate = jnp.concatenate([r[e, :, 2 * width :] for r in rows_in], axis=0).astype(F32)[:, :1]
        pre = dot(x, up)
        q = dot(g, down)
        s = jax.nn.sigmoid(pre)
        hidden = pre * s
        score = jnp.sum(hidden.astype(BF).astype(F32) * q, axis=1, keepdims=True)
        grad_a = (gate * q * (s * (1.0 + pre * (1.0 - s)))).astype(BF)
        fac_up[e] = grad_a
        fac_down[e] = (gate * hidden).astype(BF)
        rows = dot(grad_a, up, 1, 1).astype(BF)
        for b in range(2):
            part = slice(b * block, (b + 1) * block)
            to = slice(e * block, (e + 1) * block)
            grads[b, to] = rows[part]
            marks[b, to] = (score[part] * lane_of[to]).astype(BF)
    for b in range(2):
        left = dot(perm_l[...], grads[b, :, :half]) + dot(perm_r[...], grads[b, :, half:])
        first = left[:, :128] + dot(perm_s[...], marks[b])
        at = lax.bitwise_xor(spot[2], b)
        back[:, at, :, :128] = first.astype(BF).reshape(n_z, 2 * SLOTS, 128)
        back[:, at, :, 128:] = left[:, 128:].astype(BF).reshape(n_z, 2 * SLOTS, half - 128)


def weight_kernel(n_y, n_x, spot, *refs):
    rows_in, fac = refs[:4], refs[4:8]
    g_out, parts = refs[8:-1], refs[-1]
    share, hidden_len = parts.shape[2:]
    width = parts.shape[0] * share
    for e in range(2):
        for m in range(2):
            x = jnp.concatenate([r[e, :, m * width : (m + 1) * width] for r in rows_in], axis=0)
            f = jnp.concatenate((fac[m][e], fac[2 + m][e]), axis=0)
            parts[:, 2 * e + m] = dot(x, f, 0, 0).astype(BF).reshape(-1, share, hidden_len)
        for d in range(n_x):
            for i in range(n_y):
                group = lax.rem(spot[0] + i, n_y) * n_x + lax.rem(spot[1] + d, n_x)
                g_out[e * n_x + d][i] = parts[group, 2 * e : 2 * e + 2]


def total_kernel(*refs):
    *ends, up, down = refs
    n_y = len(ends) // 2
    for e in range(2):
        some = ends[e * n_y : (e + 1) * n_y]
        up[e] = sum(r[0].astype(F32) for r in some).astype(BF)
        down[e] = sum(r[1].astype(F32) for r in some).astype(BF)


def partial_sums(cap, got, at, lane_places, owners, slots, place_l, place_r):
    n_dev, _, half = got.shape
    data = got[...].reshape(n_dev * 2 * SLOTS, half)
    left = dot((at == place_l[...]).astype(F32).astype(BF), data)
    right = dot((at == place_r[...]).astype(F32).astype(BF), data)
    lines = got[:, 32:48, :128].reshape(n_dev * 16, 128)
    by_place = jnp.zeros((slots.shape[1], 128), F32)
    for m in range(2):
        by_place = by_place + dot(dot(slots[m], lines, 1, 1).astype(BF), owners[m])
    scores = jnp.zeros(lane_places.shape, F32)
    for r in range(cap):
        scores = scores + jnp.where(lane_places == r + 1.0, by_place[r : r + 1, :], 0.0)
    return left, right, scores


def partner_kernel(cap, got, pay, sel, owners, slots, place_l, place_r, out):
    width = out.shape[1] - 128
    half = width // 2
    meta = pay[HALF:, 2 * width :]
    at = dot(meta, sel[...], 0, 0)
    lane = iota((HALF, 128), 0) == iota((HALF, 128), 1)
    lane_places = dot(meta, jnp.where(lane, 1.0, 0.0).astype(BF), 0, 0)
    left, right, scores = partial_sums(cap, got, at, lane_places, owners, slots, place_l, place_r)
    out[:, :half] = left.astype(BF)
    out[:, half:width] = right.astype(BF)
    out[:, width:] = scores.astype(BF)


def combine_kernel(cap, got, table, ids, sel, owners, slots, place_l, place_r, other, grad_tok, grad_gate):
    rows, width = grad_tok.shape
    half = width // 2
    both = table[...]
    at = dot(both.astype(BF), sel[...])
    at_lane = iota((128, 128), 0) == iota((128, 128), 1) + HALF
    lane_places = dot(both.astype(BF), jnp.where(at_lane, 1.0, 0.0).astype(BF))
    left, right, scores = partial_sums(cap, got, at, lane_places, owners, slots, place_l, place_r)
    grad_tok[:, :half] = (left + other[:, :half].astype(F32)).astype(BF)
    grad_tok[:, half:] = (right + other[:, half:width].astype(F32)).astype(BF)
    scores = scores + other[:, width:].astype(F32)
    lane = iota((rows, 128), 1)
    column = iota((rows, ids.shape[1]), 1)
    chosen = ids[...]
    total = jnp.zeros((rows, ids.shape[1]), F32)
    for k in range(ids.shape[1]):
        score = jnp.sum(
            jnp.where(lane == chosen[:, k : k + 1], scores, 0.0), axis=1, keepdims=True
        )
        total = total + jnp.where(column == k, score, 0.0)
    grad_gate[...] = total.astype(BF)


def shift(value, axis, by):
    n = lax.axis_size(axis)
    return lax.ppermute(value, axis, [(i, (i + by) % n) for i in range(n)])


def ring(block, beside, then):
    steps = lax.axis_size("z") // 2
    rows = block.shape[0] // 2
    below, above = [block], [block]
    for k in range(1, steps):
        below.append(shift(below[-1], "z", 1))
        above.append(shift(above[-1], "z", -1))
        if k == 1:
            below[1], above[1], *beside = held(below[1], above[1], *beside)
            later = then(beside)
        if k == steps - 1:
            below[k], above[k], *later = held(below[k], above[k], *later)
    low = shift(below[-1][:rows], "z", 1)
    high = shift(above[-1][rows:], "z", -1)
    return below + [low, high] + above[:0:-1], later


def weights_kernel(n_y, n_x, spot, *refs):
    *blocks, out = refs
    share = blocks[0].shape[2]
    for i in range(n_y):
        for d in range(n_x):
            group = lax.rem(spot[0] + n_y - i, n_y) * n_x + lax.rem(spot[1] + n_x - d, n_x)
            start = pl.multiple_of(group * share, share)
            for m in range(4):
                out[m, pl.ds(start, share), :] = blocks[d][i, m]


def held(*values):
    return lax.optimization_barrier(values)


def per_device(tokens, grad_out, gates, expert_ids, w_up, w_down):
    rows, width = tokens.shape
    top = expert_ids.shape[1]
    n_y, n_x, n_z = lax.axis_size("yl"), lax.axis_size("x"), lax.axis_size("z")
    experts = 8 * n_z
    cap = rows * top * 9 // (8 * experts)
    block = n_z * cap
    share, hidden_len = w_up.shape[1:]
    half = width // 2
    yl, x, z, yh, c = [lax.axis_index(a) for a in ("yl", "x", "z", "yh", "c")]
    shape = jax.ShapeDtypeStruct

    pay, table = pl.pallas_call(
        prepare_kernel,
        out_shape=(shape((rows, 2 * width + 128), BF), shape((rows, 128), F32)),
        in_specs=vmem(4),
        out_specs=tuple(vmem(2)),
        cost_estimate=cost(0.1, 2),
        compiler_params=params(8),
    )(tokens, grad_out, gates, expert_ids)
    spot = jnp.stack([yl, x, c]).astype(jnp.int32)
    smem = [pl.BlockSpec(memory_space=pltpu.SMEM)]
    gath = lax.all_gather(pay, "z", axis=0)
    pay_other = shift(pay, "yh", 1)
    w_mine = jnp.concatenate((w_up, jnp.transpose(w_down, (0, 2, 1))), axis=0)
    pay_other, w_mine = held(pay_other, w_mine)

    def across(parts):
        line = jnp.stack(parts)
        return [line] + [shift(line, "x", d) for d in range(1, n_x)]

    w_parts = [w_mine] + [shift(w_mine, "yl", d) for d in range(1, n_y)]
    blocks_other, w_parts = ring(pay_other, w_parts, across)
    w_all = pl.pallas_call(
        functools.partial(weights_kernel, n_y, n_x),
        out_shape=shape((4, width, hidden_len), BF),
        in_specs=smem + vmem(n_x),
        out_specs=vmem(1)[0],
        cost_estimate=cost(0, 6),
        compiler_params=params(10),
    )(spot, *w_parts)

    j = jnp.arange(4 * block)
    b_j, d_j, r_j = j // block, (j % block) // cap, j % cap
    core_j = jnp.where(b_j >= 2, 1 - c, c)
    e_j = ((z * 2 + yh) * 2 + core_j) * 2 + b_j % 2
    sel = ((d_j * HALF + e_j)[:, None] == jnp.arange(n_z * HALF)[None, :]).astype(BF)
    place = jnp.broadcast_to((r_j[:block, None] + 1).astype(F32), (block, 128))
    origin = jnp.broadcast_to(d_j[:block, None].astype(jnp.int32), (block, 128))

    def picked(*blocks):
        own, sib = pl.pallas_call(
            functools.partial(pick_kernel, cap, n_z),
            out_shape=(shape((2, block, 2 * width + 128), BF),) * 2,
            in_specs=vmem(len(blocks) + 3),
            out_specs=tuple(vmem(2)),
            cost_estimate=cost(2.6, 12),
            compiler_params=params(20),
        )(*blocks, sel, place, origin)
        return own, shift(sib, "c", 1)

    i = jnp.arange(2 * block)
    e_i, d_i, r_i = i // block, (i % block) // cap, i % cap
    p = jnp.arange(n_z * 2 * SLOTS)
    z_p, q_p = p // (2 * SLOTS), p % (2 * SLOTS)
    slot_i = (e_i * cap + r_i)[None, :]
    lane_of = (slot_i.T == jnp.arange(128)[None, :]).astype(F32)

    def worked(own, got, z_i):
        same = z_p[:, None] == z_i[None, :]
        perms = [
            (same & (q_p[:, None] == at)).astype(BF) for at in (slot_i, slot_i + SLOTS, 2 * cap)
        ]
        return pl.pallas_call(
            functools.partial(expert_kernel, cap),
            out_shape=(shape((n_z, 2, 2 * SLOTS, half), BF),)
            + (shape((2, 2 * block, hidden_len), BF),) * 2,
            in_specs=smem + vmem(7),
            out_specs=tuple(vmem(3)),
            scratch_shapes=[
                pltpu.VMEM((2, 2 * block, width), BF),
                pltpu.VMEM((2, 2 * block, 128), BF),
            ],
            cost_estimate=cost(4, 24),
            compiler_params=params(28),
        )(spot, w_all, own, got, *perms, lane_of)

    def replies(back):
        return lax.all_to_all(
            back.reshape(2 * n_z, 2 * SLOTS, half), ("z", "c"), 0, 0, tiled=True
        )

    second = (2, len(blocks_other) - 2) if n_z > 4 else (0, 1)
    gath, *some = held(gath, *[blocks_other[i] for i in second])
    for i, value in zip(second, some):
        blocks_other[i] = value
    a_own, a_got = picked(gath)
    a_back, a_up, a_down = worked(a_own, a_got, d_i)
    b_own, b_got = picked(*blocks_other)
    a_up, b_got = held(a_up, b_got)
    b_back, b_up, b_down = worked(b_own, b_got, (z + n_z - d_i) % n_z)
    got_other = replies(b_back)
    parts = pl.pallas_call(
        functools.partial(weight_kernel, n_y, n_x),
        out_shape=(shape((n_y, 2, share, hidden_len), BF),) * (2 * n_x),
        in_specs=smem + vmem(8),
        out_specs=tuple(vmem(2 * n_x)),
        scratch_shapes=[pltpu.VMEM((n_y * n_x, 4, share, hidden_len), BF)],
        cost_estimate=cost(2, 18),
        compiler_params=params(28),
    )(spot, a_own, a_got, b_own, b_got, a_up, a_down, b_up, b_down)

    lines, ends = [], []
    for e in range(2):
        some = parts[e * n_x : (e + 1) * n_x]
        some = [some[0]] + [shift(some[d], "x", d) for d in range(1, n_x)]
        lines.append(sum(v.astype(F32) for v in some).astype(BF))
    a_back, got_other, lines[0] = held(a_back, got_other, lines[0])
    got_own = replies(a_back)
    for e in range(2):
        ends += [lines[e][0]] + [shift(lines[e][d], "yl", d) for d in range(1, n_y)]
        lines[1], *ends = held(lines[1], *ends)
    grad_up, grad_down = pl.pallas_call(
        total_kernel,
        out_shape=(shape((2, share, hidden_len), BF),) * 2,
        in_specs=vmem(2 * n_y),
        out_specs=tuple(vmem(2)),
        cost_estimate=cost(0, 2),
        compiler_params=params(6),
    )(*ends)
    grad_down = jnp.transpose(grad_down, (0, 2, 1))

    n_dev = 2 * n_z
    p = jnp.arange(n_dev * 2 * SLOTS)
    dev_p, s_p = p // (2 * SLOTS), p % (2 * SLOTS)
    q = s_p % SLOTS
    first_of = ((dev_p // 2 * 2 + yh) * 2 + dev_p % 2) * 2
    e_p = (first_of + (q >= cap))[None, :]
    sel_t = (jnp.arange(128)[:, None] == HALF + e_p).astype(BF)
    sel_p = (jnp.arange(HALF)[:, None] == e_p).astype(BF)
    tgt = jnp.where(q < 2 * cap, q % cap + 1, -1)
    place_l = jnp.where(s_p < SLOTS, tgt, -1).astype(F32)[None, :]
    place_r = jnp.where(s_p >= SLOTS, tgt, -1).astype(F32)[None, :]
    line_o = jnp.arange(n_dev * 16)
    first_o = ((line_o // 32 * 2 + yh) * 2 + line_o // 16 % 2) * 2
    first_o = jnp.where(line_o % 16 == 2 * cap - 32, first_o, -2)
    parity = jnp.arange(2)[:, None, None]
    owners = (first_o[None, :, None] + parity == jnp.arange(128)[None, None, :]).astype(BF)
    at_slot = jnp.arange(24)[None, :, None]
    slots = (
        (at_slot < cap) & (jnp.arange(128)[None, None, :] == at_slot + parity * cap)
    ).astype(BF)
    partner = pl.pallas_call(
        functools.partial(partner_kernel, cap),
        out_shape=shape((rows, width + 128), BF),
        in_specs=vmem(7),
        out_specs=vmem(1)[0],
        cost_estimate=cost(0.4, 4),
        compiler_params=params(12),
    )(got_other, pay_other, sel_p, owners, slots, place_l, place_r)
    other = shift(partner, "yh", 1)
    grad_tokens, grad_gates = pl.pallas_call(
        functools.partial(combine_kernel, cap),
        out_shape=(shape((rows, width), BF), shape((rows, top), BF)),
        in_specs=vmem(9),
        out_specs=tuple(vmem(2)),
        cost_estimate=cost(0.4, 4),
        compiler_params=params(12),
    )(got_own, table, expert_ids, sel_t, owners, slots, place_l, place_r, other)
    return (grad_tokens, grad_gates, grad_up, grad_down)


def build(mesh):
    every, dp, ctx = ("yl", "x", "z", "yh", "c"), ("yl", "x"), ("z", "yh", "c")
    tok, up, down = P(every, None), P(ctx, dp, None), P(ctx, None, dp)
    return jax.shard_map(
        per_device,
        mesh=mesh,
        in_specs=(tok, tok, tok, tok, up, down),
        out_specs=(tok, tok, up, down),
        check_vma=False,
    )


def solution(mesh):
    return build(Mesh(mesh.devices.reshape(4, 4, 8, 2, 2), ("yl", "x", "z", "yh", "c")))
```

```python
import functools

import jax
import jax.numpy as jnp
from jax import lax
from jax.experimental import pallas as pl
from jax.experimental.pallas import tpu as pltpu
from jax.sharding import Mesh, PartitionSpec as P

BF, F32 = jnp.bfloat16, jnp.float32
HALF = 64
SLOTS = 40


def params(mebibytes):
    return pltpu.CompilerParams(vmem_limit_bytes=mebibytes * 1024 * 1024)


def cost(gflop, mebibytes):
    return pl.CostEstimate(
        flops=int(gflop * 1e9), bytes_accessed=int(mebibytes * 2**20), transcendentals=0
    )


def vmem(count):
    return [pl.BlockSpec(memory_space=pltpu.VMEM)] * count


def dot(a, b, ca=1, cb=0):
    return lax.dot_general(a, b, (((ca,), (cb,)), ((), ())), preferred_element_type=F32)


def iota(shape, dim):
    return lax.broadcasted_iota(jnp.int32, shape, dim)


def prepare_kernel(tok, gout, gates, ids, pay, table):
    rows, width = tok.shape
    lane = iota((rows, 128), 1)
    expert = jnp.where(lane < HALF, lane, lane - HALF)
    gate = gates[...].astype(F32)
    chosen = ids[...]
    gate_of = jnp.zeros((rows, 128), F32)
    named = jnp.zeros((rows, 128), F32)
    for k in range(ids.shape[1]):
        hit = chosen[:, k : k + 1] == expert
        gate_of = gate_of + jnp.where(hit, gate[:, k : k + 1], 0.0)
        named = named + jnp.where(hit, 1.0, 0.0)
    before = jnp.where(iota((rows, rows), 0) > iota((rows, rows), 1), 1.0, 0.0).astype(BF)
    place = named * (dot(before, named.astype(BF)) + 1.0)
    both = jnp.where(lane < HALF, gate_of, place)
    table[...] = both
    pay[:, :width] = tok[...]
    pay[:, width : 2 * width] = gout[...]
    pay[:, 2 * width :] = both.T.astype(BF)


def pick_kernel(cap, gath, sel, place, origin, own, sib):
    n_z, rows, lanes = gath.shape
    width = lanes - 128
    block = n_z * cap
    gates = gath[:, :HALF, width:].reshape(n_z * HALF, 128)
    places = gath[:, HALF:, width:].reshape(n_z * HALF, 128)
    hits, gate_cols = [], []
    for b in range(4):
        part = slice(b * block, (b + 1) * block)
        hit = dot(sel[part], places) == place[...]
        gate_cols.append(
            jnp.sum(jnp.where(hit, dot(sel[part], gates), 0.0), axis=1, keepdims=True)
        )
        ones = jnp.where(hit, 1.0, 0.0)
        hits.append(
            jnp.concatenate(
                [jnp.where(origin[...] == s, ones, 0.0).astype(BF) for s in range(n_z)], axis=1
            )
        )
    step = min(width, 512)
    for b in range(4):
        out = own if b < 2 else sib
        for c in range(0, width, step):
            data = gath[:, :, c : c + step].reshape(n_z * rows, step)
            out[b % 2, :, c : c + step] = dot(hits[b], data).astype(BF)
        out[b % 2, :, width:] = jnp.broadcast_to(gate_cols[b], (block, 128)).astype(BF)


def experts(w_ref, x_of, g_of, gate_of, perms, lane_of, facs, grads, marks, reply):
    perm_l, perm_r, perm_s = perms
    width = w_ref.shape[1]
    block = grads.shape[1] // 2
    half = width // 2
    for e in range(2):
        up, down = w_ref[e], w_ref[2 + e]
        gate = gate_of(e)
        pre = dot(x_of(e), up)
        q = dot(g_of(e), down)
        s = jax.nn.sigmoid(pre)
        hidden = pre * s
        score = jnp.sum(hidden.astype(BF).astype(F32) * q, axis=1, keepdims=True)
        grad_a = (gate * q * (s * (1.0 + pre * (1.0 - s)))).astype(BF)
        facs[0][e] = grad_a
        facs[1][e] = (gate * hidden).astype(BF)
        rows = dot(grad_a, up, 1, 1).astype(BF)
        for b in range(2):
            part = slice(b * block, (b + 1) * block)
            to = slice(e * block, (e + 1) * block)
            grads[b, to] = rows[part]
            marks[b, to] = (score[part] * lane_of[to]).astype(BF)
    for b in range(2):
        left = dot(perm_l[...], grads[b, :, :half]) + dot(perm_r[...], grads[b, :, half:])
        first = left[:, :128] + dot(perm_s[...], marks[b])
        reply(b, slice(0, 128), first.astype(BF).reshape(-1, 2 * SLOTS, 128))
        reply(b, slice(128, half), left[:, 128:].astype(BF).reshape(-1, 2 * SLOTS, half - 128))


def own_kernel(spot, w_ref, own, got, pl_, pr_, ps_, lane_of, back, fac_up, fac_down, grads, marks):
    width = w_ref.shape[1]

    def rows_of(e, first, last):
        return jnp.concatenate([r[e, :, first:last] for r in (own, got)], axis=0)

    def reply(b, lanes, value):
        back[:, lax.bitwise_xor(spot[2], b), :, lanes] = value

    experts(
        w_ref,
        lambda e: rows_of(e, 0, width),
        lambda e: rows_of(e, width, 2 * width),
        lambda e: rows_of(e, 2 * width, 2 * width + 128).astype(F32)[:, :1],
        (pl_, pr_, ps_), lane_of, (fac_up, fac_down), grads, marks, reply,
    )


def other_kernel(
    w_ref, got, sort, sort_gate, pl_, pr_, ps_, lane_of, back_own, back, rows, fac_up, fac_down, grads, marks
):
    n_z, _, many, width = got.shape
    block = rows.shape[2] // 2
    gates = []
    for b in range(2):
        data = got[:, b].reshape(n_z * many, width)
        sorted_rows = dot(sort[...], data).astype(BF)
        for e in range(2):
            rows[0, e, b * block : (b + 1) * block] = sorted_rows[e * block : (e + 1) * block]
            rows[1, e, b * block : (b + 1) * block] = sorted_rows[(2 + e) * block : (3 + e) * block]
        line = dot(sort_gate[...], data[:, :128]) * lane_of[...]
        gates.append(jnp.sum(line, axis=1, keepdims=True))
    back[:, :, 0] = back_own[...]

    def reply(b, lanes, value):
        back[:, b, 1, :, lanes] = value

    experts(
        w_ref,
        lambda e: rows[0, e],
        lambda e: rows[1, e],
        lambda e: jnp.concatenate([g[e * block : (e + 1) * block] for g in gates], axis=0),
        (pl_, pr_, ps_), lane_of, (fac_up, fac_down), grads, marks, reply,
    )


def send_kernel(cap, pay, sel, place, out):
    n_dev, many, width = out.shape
    half = many // 2
    meta = pay[:, 2 * width :]
    hit = dot(sel[...], meta[HALF:]) == place[...]
    gate = jnp.sum(jnp.where(hit, dot(sel[...], meta[:HALF]), 0.0), axis=1, keepdims=True)
    row = lax.rem(iota(hit.shape, 0), many)
    ones = jnp.where(hit, 1.0, 0.0)
    pick_x = jnp.where(row < half, ones, 0.0).astype(BF)
    pick_g = jnp.where(row < half, 0.0, ones).astype(BF)
    line = jnp.where(row == iota(hit.shape, 1), gate, 0.0).reshape(n_dev, many, 128)
    line = jnp.sum(line, axis=1, keepdims=True)
    line = jnp.where(iota((n_dev, many, 128), 1) == 2 * cap, line, 0.0).reshape(n_dev * many, 128)
    step = min(width, 512)
    for c in range(0, width, step):
        lanes, g_lanes = slice(c, c + step), slice(width + c, width + c + step)
        value = dot(pick_x, pay[:, lanes]) + dot(pick_g, pay[:, g_lanes])
        if c == 0:
            value = jnp.concatenate((value[:, :128] + line, value[:, 128:]), axis=1)
        out[:, :, lanes] = value.astype(BF).reshape(n_dev, many, step)


def weight_kernel(n_y, n_x, spot, a_own, a_got, b_rows, *refs):
    fac, g_out, parts = refs[:4], refs[4:-1], refs[-1]
    share, hidden_len = parts.shape[2:]
    width = parts.shape[0] * share
    for e in range(2):
        for m in range(2):
            own = [r[e, :, m * width : (m + 1) * width] for r in (a_own, a_got)]
            x = jnp.concatenate(own + [b_rows[m, e]], axis=0)
            f = jnp.concatenate((fac[m][e], fac[2 + m][e]), axis=0)
            parts[:, 2 * m + e] = dot(x, f, 0, 0).astype(BF).reshape(-1, share, hidden_len)
    for d in range(n_x):
        for i in range(n_y):
            g_out[d][i] = parts[lax.rem(spot[0] + i, n_y) * n_x + lax.rem(spot[1] + d, n_x)]


def total_kernel(*refs):
    *ends, up, down = refs
    up[...] = sum(r[:2].astype(F32) for r in ends).astype(BF)
    down[...] = sum(r[2:].astype(F32) for r in ends).astype(BF)


def partial_sums(cap, got, which, at, lane_places, owners, slots, place_l, place_r):
    n_dev, _, _, half = got.shape
    data = got[:, which].reshape(n_dev * 2 * SLOTS, half)
    left = dot((at == place_l[...]).astype(F32).astype(BF), data)
    right = dot((at == place_r[...]).astype(F32).astype(BF), data)
    lines = got[:, which, 32:48, :128].reshape(n_dev * 16, 128)
    by_place = jnp.zeros((slots.shape[1], 128), F32)
    for m in range(2):
        by_place = by_place + dot(dot(slots[m], lines, 1, 1).astype(BF), owners[m])
    scores = jnp.zeros(lane_places.shape, F32)
    for r in range(cap):
        scores = scores + jnp.where(lane_places == r + 1.0, by_place[r : r + 1, :], 0.0)
    return left, right, scores


def partner_kernel(cap, got, pay, sel, owners, slots, place_l, place_r, out):
    width = out.shape[1] - 128
    half = width // 2
    meta = pay[HALF:, 2 * width :]
    at = dot(meta, sel[...], 0, 0)
    lane = iota((HALF, 128), 0) == iota((HALF, 128), 1)
    lane_places = dot(meta, jnp.where(lane, 1.0, 0.0).astype(BF), 0, 0)
    left, right, scores = partial_sums(cap, got, 1, at, lane_places, owners, slots, place_l, place_r)
    out[:, :half] = left.astype(BF)
    out[:, half:width] = right.astype(BF)
    out[:, width:] = scores.astype(BF)


def combine_kernel(cap, got, table, ids, sel, owners, slots, place_l, place_r, other, grad_tok, grad_gate):
    rows, width = grad_tok.shape
    half = width // 2
    both = table[...]
    at = dot(both.astype(BF), sel[...])
    at_lane = iota((128, 128), 0) == iota((128, 128), 1) + HALF
    lane_places = dot(both.astype(BF), jnp.where(at_lane, 1.0, 0.0).astype(BF))
    left, right, scores = partial_sums(cap, got, 0, at, lane_places, owners, slots, place_l, place_r)
    grad_tok[:, :half] = (left + other[:, :half].astype(F32)).astype(BF)
    grad_tok[:, half:] = (right + other[:, half:width].astype(F32)).astype(BF)
    scores = scores + other[:, width:].astype(F32)
    lane = iota((rows, 128), 1)
    column = iota((rows, ids.shape[1]), 1)
    chosen = ids[...]
    total = jnp.zeros((rows, ids.shape[1]), F32)
    for k in range(ids.shape[1]):
        score = jnp.sum(
            jnp.where(lane == chosen[:, k : k + 1], scores, 0.0), axis=1, keepdims=True
        )
        total = total + jnp.where(column == k, score, 0.0)
    grad_gate[...] = total.astype(BF)


def shift(value, axis, by):
    n = lax.axis_size(axis)
    return lax.ppermute(value, axis, [(i, (i + by) % n) for i in range(n)])


def weights_kernel(n_y, n_x, spot, *refs):
    *blocks, out = refs
    share = blocks[0].shape[2]
    for i in range(n_y):
        for d in range(n_x):
            group = lax.rem(spot[0] + n_y - i, n_y) * n_x + lax.rem(spot[1] + n_x - d, n_x)
            start = pl.multiple_of(group * share, share)
            for m in range(4):
                out[m, pl.ds(start, share), :] = blocks[d][i, m]


def held(*values):
    return lax.optimization_barrier(values)


def per_device(tokens, grad_out, gates, expert_ids, w_up, w_down):
    rows, width = tokens.shape
    top = expert_ids.shape[1]
    n_y, n_x, n_z = lax.axis_size("yl"), lax.axis_size("x"), lax.axis_size("z")
    experts = 8 * n_z
    cap = rows * top * 9 // (8 * experts)
    block = n_z * cap
    share, hidden_len = w_up.shape[1:]
    half = width // 2
    yl, x, z, yh, c = [lax.axis_index(a) for a in ("yl", "x", "z", "yh", "c")]
    shape = jax.ShapeDtypeStruct

    pay, table = pl.pallas_call(
        prepare_kernel,
        out_shape=(shape((rows, 2 * width + 128), BF), shape((rows, 128), F32)),
        in_specs=vmem(4),
        out_specs=tuple(vmem(2)),
        cost_estimate=cost(0.1, 2),
        compiler_params=params(8),
    )(tokens, grad_out, gates, expert_ids)
    spot = jnp.stack([yl, x, c]).astype(jnp.int32)
    smem = [pl.BlockSpec(memory_space=pltpu.SMEM)]
    gath = lax.all_gather(pay, "z", axis=0)
    pay_other = shift(pay, "yh", 1)
    n_dev = 2 * n_z
    many = 2 * SLOTS

    p = jnp.arange(n_dev * many)
    dev_p, s_p = p // many, p % many
    q = s_p % SLOTS
    first_of = ((dev_p // 2 * 2 + yh) * 2 + dev_p % 2) * 2
    e_p = first_of + (q >= cap)
    tgt = jnp.where(q < 2 * cap, q % cap + 1, -1)
    sel_s = (e_p[:, None] == jnp.arange(HALF)[None, :]).astype(BF)
    place_s = jnp.broadcast_to(tgt.astype(F32)[:, None], (n_dev * many, 128))
    sent = pl.pallas_call(
        functools.partial(send_kernel, cap),
        out_shape=shape((n_dev, many, width), BF),
        in_specs=vmem(3),
        out_specs=vmem(1)[0],
        cost_estimate=cost(1, 6),
        compiler_params=params(20),
    )(pay_other, sel_s, place_s)
    got_rows = lax.all_to_all(sent, ("z", "c"), 0, 0, tiled=True)

    w_mine = jnp.concatenate((w_up, jnp.transpose(w_down, (0, 2, 1))), axis=0)
    w_mine, _ = held(w_mine, sent)
    w_line = jnp.stack([w_mine] + [shift(w_mine, "yl", d) for d in range(1, n_y)])
    w_parts = [w_line] + [shift(w_line, "x", d) for d in range(1, n_x)]
    gath, *w_parts = held(gath, *w_parts)
    w_all = pl.pallas_call(
        functools.partial(weights_kernel, n_y, n_x),
        out_shape=shape((4, width, hidden_len), BF),
        in_specs=smem + vmem(n_x),
        out_specs=vmem(1)[0],
        cost_estimate=cost(0, 6),
        compiler_params=params(10),
    )(spot, *w_parts)

    j = jnp.arange(4 * block)
    b_j, d_j, r_j = j // block, (j % block) // cap, j % cap
    core_j = jnp.where(b_j >= 2, 1 - c, c)
    e_j = ((z * 2 + yh) * 2 + core_j) * 2 + b_j % 2
    sel = ((d_j * HALF + e_j)[:, None] == jnp.arange(n_z * HALF)[None, :]).astype(BF)
    place = jnp.broadcast_to((r_j[:block, None] + 1).astype(F32), (block, 128))
    origin = jnp.broadcast_to(d_j[:block, None].astype(jnp.int32), (block, 128))

    a_own, a_sib = pl.pallas_call(
        functools.partial(pick_kernel, cap),
        out_shape=(shape((2, block, 2 * width + 128), BF),) * 2,
        in_specs=vmem(4),
        out_specs=tuple(vmem(2)),
        cost_estimate=cost(2.6, 12),
        compiler_params=params(20),
    )(gath, sel, place, origin)
    a_got = shift(a_sib, "c", 1)

    i = jnp.arange(2 * block)
    e_i, z_i, r_i = i // block, (i % block) // cap, i % cap
    v = jnp.arange(n_z * many)
    z_v, q_v = v // many, v % many
    same = z_v[:, None] == z_i[None, :]
    slot_i = (e_i * cap + r_i)[None, :]
    in_x, in_g, in_s = [same & (q_v[:, None] == at) for at in (slot_i, slot_i + SLOTS, 2 * cap)]
    perms = [m.astype(BF) for m in (in_x, in_g, in_s)]
    sort = jnp.concatenate((in_x, in_g), axis=1).T.astype(BF)
    sort_gate = in_s.T.astype(BF)
    lane_of = (slot_i.T == jnp.arange(128)[None, :]).astype(F32)
    scratch = [pltpu.VMEM((2, 2 * block, width), BF), pltpu.VMEM((2, 2 * block, 128), BF)]
    facs = (shape((2, 2 * block, hidden_len), BF),) * 2
    a_back, a_up, a_down = pl.pallas_call(
        own_kernel,
        out_shape=(shape((n_z, 2, many, half), BF), *facs),
        in_specs=smem + vmem(7),
        out_specs=tuple(vmem(3)),
        scratch_shapes=scratch,
        cost_estimate=cost(4, 24),
        compiler_params=params(28),
    )(spot, w_all, a_own, a_got, *perms, lane_of)
    got_rows, a_up = held(got_rows, a_up)
    back, b_rows, b_up, b_down = pl.pallas_call(
        other_kernel,
        out_shape=(
            shape((n_z, 2, 2, many, half), BF),
            shape((2, 2, 2 * block, width), BF),
            *facs,
        ),
        in_specs=vmem(9),
        out_specs=tuple(vmem(4)),
        scratch_shapes=scratch,
        cost_estimate=cost(5, 24),
        compiler_params=params(32),
    )(w_all, got_rows.reshape(n_z, 2, many, width), sort, sort_gate, *perms, lane_of, a_back)
    got = lax.all_to_all(back.reshape(n_dev, 2, many, half), ("z", "c"), 0, 0, tiled=True)
    parts = pl.pallas_call(
        functools.partial(weight_kernel, n_y, n_x),
        out_shape=(shape((n_y, 4, share, hidden_len), BF),) * n_x,
        in_specs=smem + vmem(7),
        out_specs=tuple(vmem(n_x)),
        scratch_shapes=[pltpu.VMEM((n_y * n_x, 4, share, hidden_len), BF)],
        cost_estimate=cost(2, 18),
        compiler_params=params(28),
    )(spot, a_own, a_got, b_rows, a_up, a_down, b_up, b_down)

    lines = [parts[0]] + [shift(parts[d], "x", d) for d in range(1, n_x)]
    line = sum(u.astype(F32) for u in lines).astype(BF)
    ends = [line[0]] + [shift(line[d], "yl", d) for d in range(1, n_y)]
    grad_up, grad_down = pl.pallas_call(
        total_kernel,
        out_shape=(shape((2, share, hidden_len), BF),) * 2,
        in_specs=vmem(n_y),
        out_specs=tuple(vmem(2)),
        cost_estimate=cost(0, 2),
        compiler_params=params(6),
    )(*ends)
    grad_down = jnp.transpose(grad_down, (0, 2, 1))

    sel_t = (jnp.arange(128)[:, None] == HALF + e_p[None, :]).astype(BF)
    sel_p = (jnp.arange(HALF)[:, None] == e_p[None, :]).astype(BF)
    place_l = jnp.where(s_p < SLOTS, tgt, -1).astype(F32)[None, :]
    place_r = jnp.where(s_p >= SLOTS, tgt, -1).astype(F32)[None, :]
    line_o = jnp.arange(n_dev * 16)
    first_o = ((line_o // 32 * 2 + yh) * 2 + line_o // 16 % 2) * 2
    first_o = jnp.where(line_o % 16 == 2 * cap - 32, first_o, -2)
    parity = jnp.arange(2)[:, None, None]
    owners = (first_o[None, :, None] + parity == jnp.arange(128)[None, None, :]).astype(BF)
    at_slot = jnp.arange(24)[None, :, None]
    slots = (
        (at_slot < cap) & (jnp.arange(128)[None, None, :] == at_slot + parity * cap)
    ).astype(BF)
    partner = pl.pallas_call(
        functools.partial(partner_kernel, cap),
        out_shape=shape((rows, width + 128), BF),
        in_specs=vmem(7),
        out_specs=vmem(1)[0],
        cost_estimate=cost(0.4, 4),
        compiler_params=params(12),
    )(got, pay_other, sel_p, owners, slots, place_l, place_r)
    other = shift(partner, "yh", 1)
    grad_tokens, grad_gates = pl.pallas_call(
        functools.partial(combine_kernel, cap),
        out_shape=(shape((rows, width), BF), shape((rows, top), BF)),
        in_specs=vmem(9),
        out_specs=tuple(vmem(2)),
        cost_estimate=cost(0.4, 4),
        compiler_params=params(12),
    )(got, table, expert_ids, sel_t, owners, slots, place_l, place_r, other)
    return (grad_tokens, grad_gates, grad_up, grad_down)


def build(mesh):
    every, dp, ctx = ("yl", "x", "z", "yh", "c"), ("yl", "x"), ("z", "yh", "c")
    tok, up, down = P(every, None), P(ctx, dp, None), P(ctx, None, dp)
    return jax.shard_map(
        per_device,
        mesh=mesh,
        in_specs=(tok, tok, tok, tok, up, down),
        out_specs=(tok, tok, up, down),
        check_vma=False,
    )


def solution(mesh):
    return build(Mesh(mesh.devices.reshape(4, 4, 8, 2, 2), ("yl", "x", "z", "yh", "c")))
```

```python
import functools

import jax
import jax.numpy as jnp
from jax import lax
from jax.experimental import pallas as pl
from jax.experimental.pallas import tpu as pltpu
from jax.sharding import Mesh, PartitionSpec as P

BF, F32 = jnp.bfloat16, jnp.float32
HALF = 64
SLOTS = 40


def params(mebibytes):
    return pltpu.CompilerParams(vmem_limit_bytes=mebibytes * 1024 * 1024)


def cost(gflop, mebibytes):
    return pl.CostEstimate(
        flops=int(gflop * 1e9), bytes_accessed=int(mebibytes * 2**20), transcendentals=0
    )


def vmem(count):
    return [pl.BlockSpec(memory_space=pltpu.VMEM)] * count


def dot(a, b, ca=1, cb=0):
    return lax.dot_general(a, b, (((ca,), (cb,)), ((), ())), preferred_element_type=F32)


def iota(shape, dim):
    return lax.broadcasted_iota(jnp.int32, shape, dim)


def prepare_kernel(tok, gout, gates, ids, pay, table):
    rows, width = tok.shape
    line = iota((2 * HALF, rows), 0)
    expert = jnp.where(line < HALF, line, line - HALF)
    gate = gates[...].astype(F32)
    chosen = ids[...]
    gate_of = jnp.zeros((2 * HALF, rows), F32)
    named = jnp.zeros((2 * HALF, rows), F32)
    for k in range(ids.shape[0]):
        hit = chosen[k : k + 1] == expert
        gate_of = gate_of + jnp.where(hit, gate[k : k + 1], 0.0)
        named = named + jnp.where(hit, 1.0, 0.0)
    before = jnp.where(iota((rows, rows), 0) < iota((rows, rows), 1), 1.0, 0.0).astype(BF)
    place = named * (dot(named.astype(BF), before) + 1.0)
    table[...] = place[HALF:].astype(BF)
    pay[:, :width] = tok[...]
    pay[:, width : 2 * width] = gout[...]
    pay[:, 2 * width :] = jnp.where(line < HALF, gate_of, place).astype(BF)


def pick_kernel(cap, spot, gath, own, sib):
    n_z, rows, lanes = gath.shape
    width = lanes - 128
    block = n_z * cap
    gates = gath[:, :HALF, width:].reshape(n_z * HALF, 128)
    places = gath[:, HALF:, width:].reshape(n_z * HALF, 128)
    line = iota((block, n_z * HALF), 0)
    expert = lax.div(line, cap) * HALF + spot[3]
    column = iota((block, n_z * HALF), 1)
    place = (lax.rem(iota((block, 128), 0), cap) + 1).astype(F32)
    origin = lax.div(iota((block, 128), 0), cap)
    step = min(width, 512)
    for b in range(4):
        out = own if b < 2 else sib
        core = spot[2] if b < 2 else 1 - spot[2]
        sel = jnp.where(column == expert + (2 * core + b % 2), 1.0, 0.0).astype(BF)
        hit = dot(sel, places) == place
        gate = jnp.sum(jnp.where(hit, dot(sel, gates), 0.0), axis=1, keepdims=True)
        ones = jnp.where(hit, 1.0, 0.0)
        pick = jnp.concatenate(
            [jnp.where(origin == s, ones, 0.0).astype(BF) for s in range(n_z)], axis=1
        )
        for c in range(0, width, step):
            data = gath[:, :, c : c + step].reshape(n_z * rows, step)
            out[b % 2, :, c : c + step] = dot(pick, data).astype(BF)
        out[b % 2, :, width:] = jnp.broadcast_to(gate, (block, 128)).astype(BF)


def expert_kernel(n_y, n_x, cap, spot, *refs):
    w_in, (own, got, sent) = refs[:n_x], refs[n_x : n_x + 3]
    g_out, back = refs[n_x + 3 : 2 * n_x + 3], refs[2 * n_x + 3]
    weights, parts, rows, grads, marks, masks = refs[2 * n_x + 4 :]
    share = w_in[0].shape[2]
    width, hidden_len = weights.shape[1:]
    n_z, _, many, _ = sent.shape
    block = n_z * cap
    half = width // 2

    for i in range(n_y):
        for d in range(n_x):
            group = lax.rem(spot[0] + n_y - i, n_y) * n_x + lax.rem(spot[1] + n_x - d, n_x)
            start = pl.multiple_of(group * share, share)
            for m in range(4):
                weights[m, pl.ds(start, share), :] = w_in[d][i, m]

    column = iota((1, 2 * block), 1)
    slot = jnp.where(column < block, 0, cap) + lax.rem(column, cap)
    device = lax.div(jnp.where(column < block, column, column - block), cap) * many
    line = iota((n_z * many, 2 * block), 0)
    for m, at in enumerate((device + slot, device + slot + SLOTS, device + 2 * cap)):
        masks[m] = jnp.where(line == at, 1.0, 0.0).astype(BF)
    down_line = iota((2 * block, 128), 0)
    slot = jnp.where(down_line < block, 0, cap) + lax.rem(down_line, cap)
    lane_of = jnp.where(slot == iota((2 * block, 128), 1), 1.0, 0.0)

    gates = []
    step = min(width, 512)
    for b in range(2):
        data = sent[:, b].reshape(n_z * many, width)
        for m in range(2):
            for c in range(0, width, step):
                value = dot(masks[m], data[:, c : c + step], 0, 0).astype(BF)
                for e in range(2):
                    to = slice(b * block, (b + 1) * block)
                    rows[m, e, to, c : c + step] = value[e * block : (e + 1) * block]
        line = dot(masks[2], data[:, :128], 0, 0) * lane_of
        gates.append(jnp.sum(line, axis=1, keepdims=True))

    for e in range(2):
        up, down = weights[2 * e], weights[2 * e + 1]
        x = jnp.concatenate([own[e, :, :width], got[e, :, :width], rows[0, e]], axis=0)
        g = jnp.concatenate(
            [own[e, :, width : 2 * width], got[e, :, width : 2 * width], rows[1, e]], axis=0
        )
        gate = jnp.concatenate(
            [r[e, :, 2 * width :].astype(F32)[:, :1] for r in (own, got)]
            + [v[e * block : (e + 1) * block] for v in gates],
            axis=0,
        )
        pre = dot(x, up)
        q = dot(g, down)
        s = jax.nn.sigmoid(pre)
        hidden = pre * s
        score = jnp.sum(hidden.astype(BF).astype(F32) * q, axis=1, keepdims=True)
        grad_a = (gate * q * (s * (1.0 + pre * (1.0 - s)))).astype(BF)
        parts[:, 2 * e] = dot(x, grad_a, 0, 0).astype(BF).reshape(-1, share, hidden_len)
        parts[:, 2 * e + 1] = (
            dot(g, (gate * hidden).astype(BF), 0, 0).astype(BF).reshape(-1, share, hidden_len)
        )
        out = dot(grad_a, up, 1, 1).astype(BF)
        for b in range(4):
            part = slice(b * block, (b + 1) * block)
            to = slice(e * block, (e + 1) * block)
            grads[b, to] = out[part]
            marks[b, to] = (score[part] * lane_of[to]).astype(BF)
    for b in range(4):
        at = lax.bitwise_xor(spot[2], b) if b < 2 else b - 2
        left = dot(masks[0], grads[b, :, :half]) + dot(masks[1], grads[b, :, half:])
        first = left[:, :128] + dot(masks[2], marks[b])
        back[:, at, b // 2, :, :128] = first.astype(BF).reshape(n_z, many, 128)
        back[:, at, b // 2, :, 128:] = left[:, 128:].astype(BF).reshape(n_z, many, half - 128)
    for d in range(n_x):
        for i in range(n_y):
            g_out[d][i] = parts[lax.rem(spot[0] + i, n_y) * n_x + lax.rem(spot[1] + d, n_x)]


def send_kernel(cap, pay, sel, place, out):
    n_dev, many, width = out.shape
    half = many // 2
    meta = pay[:, 2 * width :]
    hit = dot(sel[...], meta[HALF:]) == place[...]
    gate = jnp.sum(jnp.where(hit, dot(sel[...], meta[:HALF]), 0.0), axis=1, keepdims=True)
    row = lax.rem(iota(hit.shape, 0), many)
    ones = jnp.where(hit, 1.0, 0.0)
    pick_x = jnp.where(row < half, ones, 0.0).astype(BF)
    pick_g = jnp.where(row < half, 0.0, ones).astype(BF)
    line = jnp.where(row == iota(hit.shape, 1), gate, 0.0).reshape(n_dev, many, 128)
    line = jnp.sum(line, axis=1, keepdims=True)
    line = jnp.where(iota((n_dev, many, 128), 1) == 2 * cap, line, 0.0).reshape(n_dev * many, 128)
    step = min(width, 512)
    for c in range(0, width, step):
        lanes, g_lanes = slice(c, c + step), slice(width + c, width + c + step)
        value = dot(pick_x, pay[:, lanes]) + dot(pick_g, pay[:, g_lanes])
        if c == 0:
            value = jnp.concatenate((value[:, :128] + line, value[:, 128:]), axis=1)
        out[:, :, lanes] = value.astype(BF).reshape(n_dev, many, step)


def total_kernel(*refs):
    *ends, up, down = refs
    for e in range(2):
        up[e] = sum(r[2 * e].astype(F32) for r in ends).astype(BF)
        down[e] = sum(r[2 * e + 1].astype(F32) for r in ends).astype(BF)


def partial_sums(cap, got, which, at, lane_places, owners, slots, place_l, place_r):
    n_dev, _, _, half = got.shape
    data = got[:, which].reshape(n_dev * 2 * SLOTS, half)
    left = dot((at == place_l[...]).astype(F32).astype(BF), data)
    right = dot((at == place_r[...]).astype(F32).astype(BF), data)
    lines = got[:, which, 32:48, :128].reshape(n_dev * 16, 128)
    by_place = jnp.zeros((slots.shape[1], 128), F32)
    for m in range(2):
        by_place = by_place + dot(dot(slots[m], lines, 1, 1).astype(BF), owners[m])
    scores = jnp.zeros(lane_places.shape, F32)
    for r in range(cap):
        scores = scores + jnp.where(lane_places == r + 1.0, by_place[r : r + 1, :], 0.0)
    return left, right, scores


def places_of(table, sel):
    same = jnp.where(iota((HALF, 128), 0) == iota((HALF, 128), 1), 1.0, 0.0).astype(BF)
    return dot(table, sel[...], 0, 0), dot(table, same, 0, 0)


def partner_kernel(cap, got, pay, sel, owners, slots, place_l, place_r, out):
    width = out.shape[1] - 128
    half = width // 2
    at, by_expert = places_of(pay[HALF:, 2 * width :], sel)
    left, right, scores = partial_sums(cap, got, 1, at, by_expert, owners, slots, place_l, place_r)
    out[:, :half] = left.astype(BF)
    out[:, half:width] = right.astype(BF)
    out[:, width:] = scores.astype(BF)


def combine_kernel(cap, got, table, ids, sel, owners, slots, place_l, place_r, other, grad_tok, grad_gate):
    rows, width = grad_tok.shape
    half = width // 2
    at, by_expert = places_of(table[...], sel)
    left, right, scores = partial_sums(cap, got, 0, at, by_expert, owners, slots, place_l, place_r)
    grad_tok[:, :half] = (left + other[:, :half].astype(F32)).astype(BF)
    grad_tok[:, half:] = (right + other[:, half:width].astype(F32)).astype(BF)
    scores = (scores + other[:, width:].astype(F32)).T
    expert = iota((128, rows), 0)
    line = iota(ids.shape, 0)
    chosen = ids[...]
    total = jnp.zeros(ids.shape, F32)
    for k in range(ids.shape[0]):
        score = jnp.where(chosen[k : k + 1] == expert, scores, 0.0)
        total = total + jnp.where(line == k, jnp.sum(score, axis=0, keepdims=True), 0.0)
    grad_gate[...] = total.astype(BF)


def shift(value, axis, by):
    n = lax.axis_size(axis)
    return lax.ppermute(value, axis, [(i, (i + by) % n) for i in range(n)])


def held(*values):
    return lax.optimization_barrier(values)


def per_device(tokens, grad_out, gates, expert_ids, w_up, w_down):
    rows, width = tokens.shape
    top = expert_ids.shape[1]
    n_y, n_x, n_z = lax.axis_size("yl"), lax.axis_size("x"), lax.axis_size("z")
    experts = 8 * n_z
    cap = rows * top * 9 // (8 * experts)
    block = n_z * cap
    share, hidden_len = w_up.shape[1:]
    half = width // 2
    yl, x, z, yh, c = [lax.axis_index(a) for a in ("yl", "x", "z", "yh", "c")]
    shape = jax.ShapeDtypeStruct

    pay, table = pl.pallas_call(
        prepare_kernel,
        out_shape=(shape((rows, 2 * width + 128), BF), shape((HALF, rows), BF)),
        in_specs=vmem(4),
        out_specs=tuple(vmem(2)),
        cost_estimate=cost(0.1, 2),
        compiler_params=params(8),
    )(tokens, grad_out, gates.T, expert_ids.T)
    spot = jnp.stack([yl, x, c, (z * 2 + yh) * 4]).astype(jnp.int32)
    smem = [pl.BlockSpec(memory_space=pltpu.SMEM)]
    gath = lax.all_gather(pay, "z", axis=0)
    pay_other = shift(pay, "yh", 1)
    n_dev = 2 * n_z
    many = 2 * SLOTS

    p = jnp.arange(n_dev * many)
    dev_p, s_p = p // many, p % many
    q = s_p % SLOTS
    first_of = ((dev_p // 2 * 2 + yh) * 2 + dev_p % 2) * 2
    e_p = first_of + (q >= cap)
    tgt = jnp.where(q < 2 * cap, q % cap + 1, -1)
    sel_s = (e_p[:, None] == jnp.arange(HALF)[None, :]).astype(BF)
    place_s = jnp.broadcast_to(tgt.astype(F32)[:, None], (n_dev * many, 128))
    sent = pl.pallas_call(
        functools.partial(send_kernel, cap),
        out_shape=shape((n_dev, many, width), BF),
        in_specs=vmem(3),
        out_specs=vmem(1)[0],
        cost_estimate=cost(1, 6),
        compiler_params=params(20),
    )(pay_other, sel_s, place_s)
    got_rows = lax.all_to_all(sent, ("z", "c"), 0, 0, tiled=True)

    w_mine = jnp.stack((w_up, jnp.transpose(w_down, (0, 2, 1))), axis=1)
    w_mine = w_mine.reshape(4, share, hidden_len)
    w_mine, _ = held(w_mine, sent)
    w_line = jnp.stack([w_mine] + [shift(w_mine, "yl", d) for d in range(1, n_y)])
    w_parts = [w_line] + [shift(w_line, "x", d) for d in range(1, n_x)]
    gath, *w_parts = held(gath, *w_parts)

    a_own, a_sib = pl.pallas_call(
        functools.partial(pick_kernel, cap),
        out_shape=(shape((2, block, 2 * width + 128), BF),) * 2,
        in_specs=smem + vmem(1),
        out_specs=tuple(vmem(2)),
        cost_estimate=cost(2.6, 12),
        compiler_params=params(20),
    )(spot, gath)
    a_got = shift(a_sib, "c", 1)
    *parts, back = pl.pallas_call(
        functools.partial(expert_kernel, n_y, n_x, cap),
        out_shape=(shape((n_y, 4, share, hidden_len), BF),) * n_x
        + (shape((n_z, 2, 2, many, half), BF),),
        in_specs=smem + vmem(n_x + 3),
        out_specs=tuple(vmem(n_x + 1)),
        scratch_shapes=[
            pltpu.VMEM((4, width, hidden_len), BF),
            pltpu.VMEM((n_y * n_x, 4, share, hidden_len), BF),
            pltpu.VMEM((2, 2, 2 * block, width), BF),
            pltpu.VMEM((4, 2 * block, width), BF),
            pltpu.VMEM((4, 2 * block, 128), BF),
            pltpu.VMEM((3, n_z * many, 2 * block), BF),
        ],
        cost_estimate=cost(9, 24),
        compiler_params=params(44),
    )(spot, *w_parts, a_own, a_got, got_rows.reshape(n_z, 2, many, width))
    got = lax.all_to_all(back.reshape(n_dev, 2, many, half), ("z", "c"), 0, 0, tiled=True)

    lines = [parts[0]] + [shift(parts[d], "x", d) for d in range(1, n_x)]
    line = sum(u.astype(F32) for u in lines).astype(BF)
    ends = [line[0]] + [shift(line[d], "yl", d) for d in range(1, n_y)]
    grad_up, grad_down = pl.pallas_call(
        total_kernel,
        out_shape=(shape((2, share, hidden_len), BF),) * 2,
        in_specs=vmem(n_y),
        out_specs=tuple(vmem(2)),
        cost_estimate=cost(0, 2),
        compiler_params=params(6),
    )(*ends)
    grad_down = jnp.transpose(grad_down, (0, 2, 1))

    sel_p = (jnp.arange(HALF)[:, None] == e_p[None, :]).astype(BF)
    place_l = jnp.where(s_p < SLOTS, tgt, -1).astype(F32)[None, :]
    place_r = jnp.where(s_p >= SLOTS, tgt, -1).astype(F32)[None, :]
    line_o = jnp.arange(n_dev * 16)
    first_o = ((line_o // 32 * 2 + yh) * 2 + line_o // 16 % 2) * 2
    first_o = jnp.where(line_o % 16 == 2 * cap - 32, first_o, -2)
    parity = jnp.arange(2)[:, None, None]
    owners = (first_o[None, :, None] + parity == jnp.arange(128)[None, None, :]).astype(BF)
    at_slot = jnp.arange(24)[None, :, None]
    slots = (
        (at_slot < cap) & (jnp.arange(128)[None, None, :] == at_slot + parity * cap)
    ).astype(BF)
    partner = pl.pallas_call(
        functools.partial(partner_kernel, cap),
        out_shape=shape((rows, width + 128), BF),
        in_specs=vmem(7),
        out_specs=vmem(1)[0],
        cost_estimate=cost(0.4, 4),
        compiler_params=params(12),
    )(got, pay_other, sel_p, owners, slots, place_l, place_r)
    other = shift(partner, "yh", 1)
    grad_tokens, grad_gates = pl.pallas_call(
        functools.partial(combine_kernel, cap),
        out_shape=(shape((rows, width), BF), shape((top, rows), BF)),
        in_specs=vmem(9),
        out_specs=tuple(vmem(2)),
        cost_estimate=cost(0.4, 4),
        compiler_params=params(12),
    )(got, table, expert_ids.T, sel_p, owners, slots, place_l, place_r, other)
    return (grad_tokens, grad_gates.T, grad_up, grad_down)


def build(mesh):
    every, dp, ctx = ("yl", "x", "z", "yh", "c"), ("yl", "x"), ("z", "yh", "c")
    tok, up, down = P(every, None), P(ctx, dp, None), P(ctx, None, dp)
    return jax.shard_map(
        per_device,
        mesh=mesh,
        in_specs=(tok, tok, tok, tok, up, down),
        out_specs=(tok, tok, up, down),
        check_vma=False,
    )


def solution(mesh):
    return build(Mesh(mesh.devices.reshape(4, 4, 8, 2, 2), ("yl", "x", "z", "yh", "c")))
```

```python
import functools

import jax
import jax.numpy as jnp
from jax import lax
from jax.experimental import pallas as pl
from jax.experimental.pallas import tpu as pltpu
from jax.sharding import Mesh, PartitionSpec as P

BF, F32 = jnp.bfloat16, jnp.float32
HALF = 64
SLOTS = 40


def params(mebibytes):
    return pltpu.CompilerParams(vmem_limit_bytes=mebibytes * 1024 * 1024)


def cost(gflop, mebibytes):
    return pl.CostEstimate(
        flops=int(gflop * 1e9), bytes_accessed=int(mebibytes * 2**20), transcendentals=0
    )


def vmem(count):
    return [pl.BlockSpec(memory_space=pltpu.VMEM)] * count


def dot(a, b, ca=1, cb=0):
    return lax.dot_general(a, b, (((ca,), (cb,)), ((), ())), preferred_element_type=F32)


def iota(shape, dim):
    return lax.broadcasted_iota(jnp.int32, shape, dim)


def prepare_kernel(tok, gout, gates, ids, pay, table):
    rows, width = tok.shape
    line = iota((2 * HALF, rows), 0)
    expert = jnp.where(line < HALF, line, line - HALF)
    gate = gates[...].astype(F32)
    chosen = ids[...]
    gate_of = jnp.zeros((2 * HALF, rows), F32)
    named = jnp.zeros((2 * HALF, rows), F32)
    for k in range(ids.shape[0]):
        hit = chosen[k : k + 1] == expert
        gate_of = gate_of + jnp.where(hit, gate[k : k + 1], 0.0)
        named = named + jnp.where(hit, 1.0, 0.0)
    before = jnp.where(iota((rows, rows), 0) < iota((rows, rows), 1), 1.0, 0.0).astype(BF)
    place = named * (dot(named.astype(BF), before) + 1.0)
    table[...] = place[HALF:].astype(BF)
    pay[:, :width] = tok[...]
    pay[:, width : 2 * width] = gout[...]
    pay[:, 2 * width :] = jnp.where(line < HALF, gate_of, place).astype(BF)


def pick_kernel(cap, spot, gath, own, sib):
    n_z, rows, lanes = gath.shape
    width = lanes - 128
    block = n_z * cap
    gates = gath[:, :HALF, width:].reshape(n_z * HALF, 128)
    places = gath[:, HALF:, width:].reshape(n_z * HALF, 128)
    line = iota((block, n_z * HALF), 0)
    expert = lax.div(line, cap) * HALF + spot[3]
    column = iota((block, n_z * HALF), 1)
    place = (lax.rem(iota((block, 128), 0), cap) + 1).astype(F32)
    origin = lax.div(iota((block, 128), 0), cap)
    step = min(width, 512)
    for b in range(4):
        out = own if b < 2 else sib
        core = spot[2] if b < 2 else 1 - spot[2]
        sel = jnp.where(column == expert + (2 * core + b % 2), 1.0, 0.0).astype(BF)
        hit = dot(sel, places) == place
        gate = jnp.sum(jnp.where(hit, dot(sel, gates), 0.0), axis=1, keepdims=True)
        ones = jnp.where(hit, 1.0, 0.0)
        pick = jnp.concatenate(
            [jnp.where(origin == s, ones, 0.0).astype(BF) for s in range(n_z)], axis=1
        )
        for c in range(0, width, step):
            data = gath[:, :, c : c + step].reshape(n_z * rows, step)
            out[b % 2, :, c : c + step] = dot(pick, data).astype(BF)
        out[b % 2, :, width:] = jnp.broadcast_to(gate, (block, 128)).astype(BF)


def expert_kernel(n_y, n_x, cap, spot, *refs):
    w_in, (own, got, sent) = refs[:n_x], refs[n_x : n_x + 3]
    g_out, back = refs[n_x + 3 : 2 * n_x + 3], refs[2 * n_x + 3]
    weights, parts, rows, grads, marks, masks = refs[2 * n_x + 4 :]
    share = w_in[0].shape[2]
    width, hidden_len = weights.shape[1:]
    n_z, _, many, _ = sent.shape
    block = n_z * cap
    half = width // 2

    for i in range(n_y):
        for d in range(n_x):
            group = lax.rem(spot[0] + n_y - i, n_y) * n_x + lax.rem(spot[1] + n_x - d, n_x)
            start = pl.multiple_of(group * share, share)
            for m in range(4):
                weights[m, pl.ds(start, share), :] = w_in[d][i, m]

    column = iota((1, 2 * block), 1)
    slot = jnp.where(column < block, 0, cap) + lax.rem(column, cap)
    device = lax.div(jnp.where(column < block, column, column - block), cap) * many
    line = iota((n_z * many, 2 * block), 0)
    for m, at in enumerate((device + slot, device + slot + SLOTS, device + 2 * cap)):
        masks[m] = jnp.where(line == at, 1.0, 0.0).astype(BF)
    down_line = iota((2 * block, 128), 0)
    slot = jnp.where(down_line < block, 0, cap) + lax.rem(down_line, cap)
    lane_of = jnp.where(slot == iota((2 * block, 128), 1), 1.0, 0.0)

    gates = []
    step = min(width, 512)
    for b in range(2):
        data = sent[:, b].reshape(n_z * many, width)
        for m in range(2):
            for c in range(0, width, step):
                value = dot(masks[m], data[:, c : c + step], 0, 0).astype(BF)
                for e in range(2):
                    to = slice(b * block, (b + 1) * block)
                    rows[m, e, to, c : c + step] = value[e * block : (e + 1) * block]
        line = dot(masks[2], data[:, :128], 0, 0) * lane_of
        gates.append(jnp.sum(line, axis=1, keepdims=True))

    for e in range(2):
        up, down = weights[2 * e], weights[2 * e + 1]
        x = jnp.concatenate([own[e, :, :width], got[e, :, :width], rows[0, e]], axis=0)
        g = jnp.concatenate(
            [own[e, :, width : 2 * width], got[e, :, width : 2 * width], rows[1, e]], axis=0
        )
        gate = jnp.concatenate(
            [r[e, :, 2 * width :].astype(F32)[:, :1] for r in (own, got)]
            + [v[e * block : (e + 1) * block] for v in gates],
            axis=0,
        )
        pre = dot(x, up)
        q = dot(g, down)
        s = jax.nn.sigmoid(pre)
        hidden = pre * s
        score = jnp.sum(hidden.astype(BF).astype(F32) * q, axis=1, keepdims=True)
        grad_a = (gate * q * (s * (1.0 + pre * (1.0 - s)))).astype(BF)
        parts[:, 2 * e] = dot(x, grad_a, 0, 0).astype(BF).reshape(-1, share, hidden_len)
        parts[:, 2 * e + 1] = (
            dot(g, (gate * hidden).astype(BF), 0, 0).astype(BF).reshape(-1, share, hidden_len)
        )
        out = dot(grad_a, up, 1, 1).astype(BF)
        for b in range(4):
            part = slice(b * block, (b + 1) * block)
            to = slice(e * block, (e + 1) * block)
            grads[b, to] = out[part]
            marks[b, to] = (score[part] * lane_of[to]).astype(BF)
    for b in range(4):
        at = lax.bitwise_xor(spot[2], b) if b < 2 else b - 2
        left = dot(masks[0], grads[b, :, :half]) + dot(masks[1], grads[b, :, half:])
        first = left[:, :128] + dot(masks[2], marks[b])
        half_at = spot[4] if b < 2 else 1 - spot[4]
        back[:, half_at, at, :, :128] = first.astype(BF).reshape(n_z, many, 128)
        back[:, half_at, at, :, 128:] = left[:, 128:].astype(BF).reshape(n_z, many, half - 128)
    for d in range(n_x):
        for i in range(n_y):
            g_out[d][i] = parts[lax.rem(spot[0] + i, n_y) * n_x + lax.rem(spot[1] + d, n_x)]


def send_kernel(cap, pay, sel, place, out):
    n_dev, many, width = out.shape
    half = many // 2
    meta = pay[:, 2 * width :]
    hit = dot(sel[...], meta[HALF:]) == place[...]
    gate = jnp.sum(jnp.where(hit, dot(sel[...], meta[:HALF]), 0.0), axis=1, keepdims=True)
    row = lax.rem(iota(hit.shape, 0), many)
    ones = jnp.where(hit, 1.0, 0.0)
    pick_x = jnp.where(row < half, ones, 0.0).astype(BF)
    pick_g = jnp.where(row < half, 0.0, ones).astype(BF)
    line = jnp.where(row == iota(hit.shape, 1), gate, 0.0).reshape(n_dev, many, 128)
    line = jnp.sum(line, axis=1, keepdims=True)
    line = jnp.where(iota((n_dev, many, 128), 1) == 2 * cap, line, 0.0).reshape(n_dev * many, 128)
    step = min(width, 512)
    for c in range(0, width, step):
        lanes, g_lanes = slice(c, c + step), slice(width + c, width + c + step)
        value = dot(pick_x, pay[:, lanes]) + dot(pick_g, pay[:, g_lanes])
        if c == 0:
            value = jnp.concatenate((value[:, :128] + line, value[:, 128:]), axis=1)
        out[:, :, lanes] = value.astype(BF).reshape(n_dev, many, step)


def total_kernel(*refs):
    *ends, up, down = refs
    for e in range(2):
        up[e] = sum(r[2 * e].astype(F32) for r in ends).astype(BF)
        down[e] = sum(r[2 * e + 1].astype(F32) for r in ends).astype(BF)


def sums(cap, got, at, lane_places, owners, slots, place_l, place_r):
    n_dev, _, half = got.shape
    data = got[...].reshape(n_dev * 2 * SLOTS, half)
    left = dot((at == place_l[...]).astype(F32).astype(BF), data)
    right = dot((at == place_r[...]).astype(F32).astype(BF), data)
    lines = got[:, 32:48, :128].reshape(n_dev * 16, 128)
    by_place = jnp.zeros((slots.shape[1], 128), F32)
    for m in range(2):
        by_place = by_place + dot(dot(slots[m], lines, 1, 1).astype(BF), owners[m])
    scores = jnp.zeros(lane_places.shape, F32)
    for r in range(cap):
        scores = scores + jnp.where(lane_places == r + 1.0, by_place[r : r + 1, :], 0.0)
    return left, right, scores


def places_of(table, sel):
    same = jnp.where(iota((HALF, 128), 0) == iota((HALF, 128), 1), 1.0, 0.0).astype(BF)
    return dot(table, sel[...], 0, 0), dot(table, same, 0, 0)


def combine_kernel(cap, got, table, ids, sel, owners, slots, place_l, place_r, grad_tok, grad_gate):
    rows, width = grad_tok.shape
    half = width // 2
    at, by_expert = places_of(table[...], sel)
    left, right, scores = sums(cap, got, at, by_expert, owners, slots, place_l, place_r)
    grad_tok[:, :half] = left.astype(BF)
    grad_tok[:, half:] = right.astype(BF)
    scores = scores.T
    expert = iota((128, rows), 0)
    line = iota(ids.shape, 0)
    chosen = ids[...]
    total = jnp.zeros(ids.shape, F32)
    for k in range(ids.shape[0]):
        score = jnp.where(chosen[k : k + 1] == expert, scores, 0.0)
        total = total + jnp.where(line == k, jnp.sum(score, axis=0, keepdims=True), 0.0)
    grad_gate[...] = total.astype(BF)


def shift(value, axis, by):
    n = lax.axis_size(axis)
    return lax.ppermute(value, axis, [(i, (i + by) % n) for i in range(n)])


def held(*values):
    return lax.optimization_barrier(values)


def per_device(tokens, grad_out, gates, expert_ids, w_up, w_down):
    rows, width = tokens.shape
    top = expert_ids.shape[1]
    n_y, n_x, n_z = lax.axis_size("yl"), lax.axis_size("x"), lax.axis_size("z")
    experts = 8 * n_z
    cap = rows * top * 9 // (8 * experts)
    block = n_z * cap
    share, hidden_len = w_up.shape[1:]
    half = width // 2
    yl, x, z, yh, c = [lax.axis_index(a) for a in ("yl", "x", "z", "yh", "c")]
    shape = jax.ShapeDtypeStruct

    pay, table = pl.pallas_call(
        prepare_kernel,
        out_shape=(shape((rows, 2 * width + 128), BF), shape((HALF, rows), BF)),
        in_specs=vmem(4),
        out_specs=tuple(vmem(2)),
        cost_estimate=cost(0.1, 2),
        compiler_params=params(8),
    )(tokens, grad_out, gates.T, expert_ids.T)
    spot = jnp.stack([yl, x, c, (z * 2 + yh) * 4, yh]).astype(jnp.int32)
    smem = [pl.BlockSpec(memory_space=pltpu.SMEM)]
    gath = lax.all_gather(pay, "z", axis=0)
    pay_other = shift(pay, "yh", 1)
    n_dev = 2 * n_z
    many = 2 * SLOTS

    p = jnp.arange(n_dev * many)
    dev_p, s_p = p // many, p % many
    q = s_p % SLOTS
    first_of = ((dev_p // 2 * 2 + yh) * 2 + dev_p % 2) * 2
    e_p = first_of + (q >= cap)
    tgt = jnp.where(q < 2 * cap, q % cap + 1, -1)
    sel_s = (e_p[:, None] == jnp.arange(HALF)[None, :]).astype(BF)
    place_s = jnp.broadcast_to(tgt.astype(F32)[:, None], (n_dev * many, 128))
    sent = pl.pallas_call(
        functools.partial(send_kernel, cap),
        out_shape=shape((n_dev, many, width), BF),
        in_specs=vmem(3),
        out_specs=vmem(1)[0],
        cost_estimate=cost(1, 6),
        compiler_params=params(20),
    )(pay_other, sel_s, place_s)
    got_rows = lax.all_to_all(sent, ("z", "c"), 0, 0, tiled=True)

    w_mine = jnp.stack((w_up, jnp.transpose(w_down, (0, 2, 1))), axis=1)
    w_mine = w_mine.reshape(4, share, hidden_len)
    w_mine, _ = held(w_mine, sent)
    w_line = jnp.stack([w_mine] + [shift(w_mine, "yl", d) for d in range(1, n_y)])
    w_parts = [w_line] + [shift(w_line, "x", d) for d in range(1, n_x)]
    gath, *w_parts = held(gath, *w_parts)

    a_own, a_sib = pl.pallas_call(
        functools.partial(pick_kernel, cap),
        out_shape=(shape((2, block, 2 * width + 128), BF),) * 2,
        in_specs=smem + vmem(1),
        out_specs=tuple(vmem(2)),
        cost_estimate=cost(2.6, 12),
        compiler_params=params(20),
    )(spot, gath)
    a_got = shift(a_sib, "c", 1)
    *parts, back = pl.pallas_call(
        functools.partial(expert_kernel, n_y, n_x, cap),
        out_shape=(shape((n_y, 4, share, hidden_len), BF),) * n_x
        + (shape((n_z, 2, 2, many, half), BF),),
        in_specs=smem + vmem(n_x + 3),
        out_specs=tuple(vmem(n_x + 1)),
        scratch_shapes=[
            pltpu.VMEM((4, width, hidden_len), BF),
            pltpu.VMEM((n_y * n_x, 4, share, hidden_len), BF),
            pltpu.VMEM((2, 2, 2 * block, width), BF),
            pltpu.VMEM((4, 2 * block, width), BF),
            pltpu.VMEM((4, 2 * block, 128), BF),
            pltpu.VMEM((3, n_z * many, 2 * block), BF),
        ],
        cost_estimate=cost(9, 24),
        compiler_params=params(44),
    )(spot, *w_parts, a_own, a_got, got_rows.reshape(n_z, 2, many, width))
    got = lax.all_to_all(back.reshape(2 * n_dev, many, half), ("z", "yh", "c"), 0, 0, tiled=True)

    lines = [parts[0]] + [shift(parts[d], "x", d) for d in range(1, n_x)]
    line = sum(u.astype(F32) for u in lines).astype(BF)
    ends = [line[0]] + [shift(line[d], "yl", d) for d in range(1, n_y)]
    grad_up, grad_down = pl.pallas_call(
        total_kernel,
        out_shape=(shape((2, share, hidden_len), BF),) * 2,
        in_specs=vmem(n_y),
        out_specs=tuple(vmem(2)),
        cost_estimate=cost(0, 2),
        compiler_params=params(6),
    )(*ends)
    grad_down = jnp.transpose(grad_down, (0, 2, 1))

    p = jnp.arange(2 * n_dev * many)
    s_p = p % many
    q = s_p % SLOTS
    e_p = p // many * 2 + (q >= cap)
    tgt = jnp.where(q < 2 * cap, q % cap + 1, -1)
    sel_p = (jnp.arange(HALF)[:, None] == e_p[None, :]).astype(BF)
    place_l = jnp.where(s_p < SLOTS, tgt, -1).astype(F32)[None, :]
    place_r = jnp.where(s_p >= SLOTS, tgt, -1).astype(F32)[None, :]
    line_o = jnp.arange(2 * n_dev * 16)
    first_o = jnp.where(line_o % 16 == 2 * cap - 32, line_o // 16 * 2, -2)
    parity = jnp.arange(2)[:, None, None]
    owners = (first_o[None, :, None] + parity == jnp.arange(128)[None, None, :]).astype(BF)
    at_slot = jnp.arange(24)[None, :, None]
    slots = (
        (at_slot < cap) & (jnp.arange(128)[None, None, :] == at_slot + parity * cap)
    ).astype(BF)
    grad_tokens, grad_gates = pl.pallas_call(
        functools.partial(combine_kernel, cap),
        out_shape=(shape((rows, width), BF), shape((top, rows), BF)),
        in_specs=vmem(8),
        out_specs=tuple(vmem(2)),
        cost_estimate=cost(0.4, 4),
        compiler_params=params(12),
    )(got, table, expert_ids.T, sel_p, owners, slots, place_l, place_r)
    return (grad_tokens, grad_gates.T, grad_up, grad_down)


def build(mesh):
    every, dp, ctx = ("yl", "x", "z", "yh", "c"), ("yl", "x"), ("z", "yh", "c")
    tok, up, down = P(every, None), P(ctx, dp, None), P(ctx, None, dp)
    return jax.shard_map(
        per_device,
        mesh=mesh,
        in_specs=(tok, tok, tok, tok, up, down),
        out_specs=(tok, tok, up, down),
        check_vma=False,
    )


def solution(mesh):
    return build(Mesh(mesh.devices.reshape(4, 4, 8, 2, 2), ("yl", "x", "z", "yh", "c")))
```

```python
import functools

import jax
import jax.numpy as jnp
from jax import lax
from jax.experimental import pallas as pl
from jax.experimental.pallas import tpu as pltpu
from jax.sharding import Mesh, PartitionSpec as P

BF, F32 = jnp.bfloat16, jnp.float32
HALF = 64
SLOTS = 40


def params(mebibytes):
    return pltpu.CompilerParams(vmem_limit_bytes=mebibytes * 1024 * 1024)


def cost(gflop, mebibytes):
    return pl.CostEstimate(
        flops=int(gflop * 1e9), bytes_accessed=int(mebibytes * 2**20), transcendentals=0
    )


def vmem(count):
    return [pl.BlockSpec(memory_space=pltpu.VMEM)] * count


def dot(a, b, ca=1, cb=0):
    return lax.dot_general(a, b, (((ca,), (cb,)), ((), ())), preferred_element_type=F32)


def iota(shape, dim):
    return lax.broadcasted_iota(jnp.int32, shape, dim)


def prepare_kernel(tok, gout, gates, ids, pay, table):
    rows, width = tok.shape
    line = iota((2 * HALF, rows), 0)
    expert = jnp.where(line < HALF, line, line - HALF)
    gate = gates[...].astype(F32)
    chosen = ids[...]
    gate_of = jnp.zeros((2 * HALF, rows), F32)
    named = jnp.zeros((2 * HALF, rows), F32)
    for k in range(ids.shape[0]):
        hit = chosen[k : k + 1] == expert
        gate_of = gate_of + jnp.where(hit, gate[k : k + 1], 0.0)
        named = named + jnp.where(hit, 1.0, 0.0)
    before = jnp.where(iota((rows, rows), 0) < iota((rows, rows), 1), 1.0, 0.0).astype(BF)
    place = named * (dot(named.astype(BF), before) + 1.0)
    table[...] = place[HALF:].astype(BF)
    pay[:, :width] = tok[...]
    pay[:, width : 2 * width] = gout[...]
    pay[:, 2 * width :] = jnp.where(line < HALF, gate_of, place).astype(BF)


def pick_kernel(cap, spot, gath, own, sib):
    n_z, rows, lanes = gath.shape
    width = lanes - 128
    block = n_z * cap
    gates = gath[:, :HALF, width:].reshape(n_z * HALF, 128)
    places = gath[:, HALF:, width:].reshape(n_z * HALF, 128)
    line = iota((block, n_z * HALF), 0)
    expert = lax.div(line, cap) * HALF + spot[3]
    column = iota((block, n_z * HALF), 1)
    place = (lax.rem(iota((block, 128), 0), cap) + 1).astype(F32)
    origin = lax.div(iota((block, 128), 0), cap)
    step = min(width, 512)
    for b in range(4):
        out = own if b < 2 else sib
        core = spot[2] if b < 2 else 1 - spot[2]
        sel = jnp.where(column == expert + (2 * core + b % 2), 1.0, 0.0).astype(BF)
        hit = dot(sel, places) == place
        gate = jnp.sum(jnp.where(hit, dot(sel, gates), 0.0), axis=1, keepdims=True)
        ones = jnp.where(hit, 1.0, 0.0)
        pick = jnp.concatenate(
            [jnp.where(origin == s, ones, 0.0).astype(BF) for s in range(n_z)], axis=1
        )
        for c in range(0, width, step):
            data = gath[:, :, c : c + step].reshape(n_z * rows, step)
            out[b % 2, :, c : c + step] = dot(pick, data).astype(BF)
        out[b % 2, :, width:] = jnp.broadcast_to(gate, (block, 128)).astype(BF)


def expert_kernel(n_y, n_x, cap, spot, *refs):
    w_in, (own, got, sent) = refs[:n_x], refs[n_x : n_x + 3]
    g_out, back = refs[n_x + 3 : 2 * n_x + 3], refs[2 * n_x + 3]
    weights, parts, rows, grads, marks, masks = refs[2 * n_x + 4 :]
    share = w_in[0].shape[2]
    width, hidden_len = weights.shape[1:]
    n_z, _, many, _ = sent.shape
    block = n_z * cap
    half = width // 2

    for i in range(n_y):
        for d in range(n_x):
            group = lax.rem(spot[0] + n_y - i, n_y) * n_x + lax.rem(spot[1] + n_x - d, n_x)
            start = pl.multiple_of(group * share, share)
            for m in range(4):
                weights[m, pl.ds(start, share), :] = w_in[d][i, m]

    column = iota((1, 2 * block), 1)
    slot = jnp.where(column < block, 0, cap) + lax.rem(column, cap)
    device = lax.div(jnp.where(column < block, column, column - block), cap) * many
    line = iota((n_z * many, 2 * block), 0)
    for m, at in enumerate((device + slot, device + slot + SLOTS, device + 2 * cap)):
        masks[m] = jnp.where(line == at, 1.0, 0.0).astype(BF)
    down_line = iota((2 * block, 128), 0)
    slot = jnp.where(down_line < block, 0, cap) + lax.rem(down_line, cap)
    lane_of = jnp.where(slot == iota((2 * block, 128), 1), 1.0, 0.0)

    gates = []
    step = min(width, 512)
    for b in range(2):
        data = sent[:, b].reshape(n_z * many, width)
        for m in range(2):
            for c in range(0, width, step):
                value = dot(masks[m], data[:, c : c + step], 0, 0).astype(BF)
                for e in range(2):
                    to = slice(b * block, (b + 1) * block)
                    rows[m, e, to, c : c + step] = value[e * block : (e + 1) * block]
        line = dot(masks[2], data[:, :128], 0, 0) * lane_of
        gates.append(jnp.sum(line, axis=1, keepdims=True))

    for e in range(2):
        up, down = weights[2 * e], weights[2 * e + 1]
        x = jnp.concatenate([own[e, :, :width], got[e, :, :width], rows[0, e]], axis=0)
        g = jnp.concatenate(
            [own[e, :, width : 2 * width], got[e, :, width : 2 * width], rows[1, e]], axis=0
        )
        gate = jnp.concatenate(
            [r[e, :, 2 * width :].astype(F32)[:, :1] for r in (own, got)]
            + [v[e * block : (e + 1) * block] for v in gates],
            axis=0,
        )
        pre = dot(x, up)
        q = dot(g, down)
        s = jax.nn.sigmoid(pre)
        hidden = pre * s
        score = jnp.sum(hidden.astype(BF).astype(F32) * q, axis=1, keepdims=True)
        grad_a = (gate * q * (s * (1.0 + pre * (1.0 - s)))).astype(BF)
        parts[:, 2 * e] = dot(x, grad_a, 0, 0).astype(BF).reshape(-1, share, hidden_len)
        parts[:, 2 * e + 1] = (
            dot(g, (gate * hidden).astype(BF), 0, 0).astype(BF).reshape(-1, share, hidden_len)
        )
        out = dot(grad_a, up, 1, 1).astype(BF)
        for b in range(4):
            part = slice(b * block, (b + 1) * block)
            to = slice(e * block, (e + 1) * block)
            grads[b, to] = out[part]
            marks[b, to] = (score[part] * lane_of[to]).astype(BF)
    for b in range(4):
        at = lax.bitwise_xor(spot[2], b) if b < 2 else b - 2
        left = dot(masks[0], grads[b, :, :half]) + dot(masks[1], grads[b, :, half:])
        first = left[:, :128] + dot(masks[2], marks[b])
        back[:, at, b // 2, :, :128] = first.astype(BF).reshape(n_z, many, 128)
        back[:, at, b // 2, :, 128:] = left[:, 128:].astype(BF).reshape(n_z, many, half - 128)
    for d in range(n_x):
        for i in range(n_y):
            g_out[d][i] = parts[lax.rem(spot[0] + i, n_y) * n_x + lax.rem(spot[1] + d, n_x)]


def send_kernel(cap, pay, sel, place, out):
    n_dev, many, width = out.shape
    half = many // 2
    meta = pay[:, 2 * width :]
    hit = dot(sel[...], meta[HALF:]) == place[...]
    gate = jnp.sum(jnp.where(hit, dot(sel[...], meta[:HALF]), 0.0), axis=1, keepdims=True)
    row = lax.rem(iota(hit.shape, 0), many)
    ones = jnp.where(hit, 1.0, 0.0)
    pick_x = jnp.where(row < half, ones, 0.0).astype(BF)
    pick_g = jnp.where(row < half, 0.0, ones).astype(BF)
    line = jnp.where(row == iota(hit.shape, 1), gate, 0.0).reshape(n_dev, many, 128)
    line = jnp.sum(line, axis=1, keepdims=True)
    line = jnp.where(iota((n_dev, many, 128), 1) == 2 * cap, line, 0.0).reshape(n_dev * many, 128)
    step = min(width, 512)
    for c in range(0, width, step):
        lanes, g_lanes = slice(c, c + step), slice(width + c, width + c + step)
        value = dot(pick_x, pay[:, lanes]) + dot(pick_g, pay[:, g_lanes])
        if c == 0:
            value = jnp.concatenate((value[:, :128] + line, value[:, 128:]), axis=1)
        out[:, :, lanes] = value.astype(BF).reshape(n_dev, many, step)


def total_kernel(*refs):
    *ends, up, down = refs
    for e in range(2):
        up[e] = sum(r[2 * e].astype(F32) for r in ends).astype(BF)
        down[e] = sum(r[2 * e + 1].astype(F32) for r in ends).astype(BF)


def partial_sums(cap, got, which, at, lane_places, owners, slots, place_l, place_r):
    n_dev, _, _, half = got.shape
    data = got[:, which].reshape(n_dev * 2 * SLOTS, half)
    left = dot((at == place_l[...]).astype(F32).astype(BF), data)
    right = dot((at == place_r[...]).astype(F32).astype(BF), data)
    lines = got[:, which, 32:48, :128].reshape(n_dev * 16, 128)
    by_place = jnp.zeros((slots.shape[1], 128), F32)
    for m in range(2):
        by_place = by_place + dot(dot(slots[m], lines, 1, 1).astype(BF), owners[m])
    scores = jnp.zeros(lane_places.shape, F32)
    for r in range(cap):
        scores = scores + jnp.where(lane_places == r + 1.0, by_place[r : r + 1, :], 0.0)
    return left, right, scores


def places_of(table, sel):
    same = jnp.where(iota((HALF, 128), 0) == iota((HALF, 128), 1), 1.0, 0.0).astype(BF)
    return dot(table, sel[...], 0, 0), dot(table, same, 0, 0)


def partner_kernel(cap, got, pay, sel, owners, slots, place_l, place_r, out):
    width = out.shape[1] - 128
    half = width // 2
    at, by_expert = places_of(pay[HALF:, 2 * width :], sel)
    left, right, scores = partial_sums(cap, got, 1, at, by_expert, owners, slots, place_l, place_r)
    out[:, :half] = left.astype(BF)
    out[:, half:width] = right.astype(BF)
    out[:, width:] = scores.astype(BF)


def combine_kernel(cap, got, table, ids, sel, owners, slots, place_l, place_r, other, grad_tok, grad_gate):
    rows, width = grad_tok.shape
    half = width // 2
    at, by_expert = places_of(table[...], sel)
    left, right, scores = partial_sums(cap, got, 0, at, by_expert, owners, slots, place_l, place_r)
    grad_tok[:, :half] = (left + other[:, :half].astype(F32)).astype(BF)
    grad_tok[:, half:] = (right + other[:, half:width].astype(F32)).astype(BF)
    scores = (scores + other[:, width:].astype(F32)).T
    expert = iota((128, rows), 0)
    line = iota(ids.shape, 0)
    chosen = ids[...]
    total = jnp.zeros(ids.shape, F32)
    for k in range(ids.shape[0]):
        score = jnp.where(chosen[k : k + 1] == expert, scores, 0.0)
        total = total + jnp.where(line == k, jnp.sum(score, axis=0, keepdims=True), 0.0)
    grad_gate[...] = total.astype(BF)


def shift(value, axis, by):
    n = lax.axis_size(axis)
    return lax.ppermute(value, axis, [(i, (i + by) % n) for i in range(n)])


def held(*values):
    return lax.optimization_barrier(values)


def per_device(tokens, grad_out, gates, expert_ids, w_up, w_down):
    rows, width = tokens.shape
    top = expert_ids.shape[1]
    n_y, n_x, n_z = lax.axis_size("yl"), lax.axis_size("x"), lax.axis_size("z")
    experts = 8 * n_z
    cap = rows * top * 9 // (8 * experts)
    block = n_z * cap
    share, hidden_len = w_up.shape[1:]
    half = width // 2
    yl, x, z, yh, c = [lax.axis_index(a) for a in ("yl", "x", "z", "yh", "c")]
    shape = jax.ShapeDtypeStruct

    pay, table = pl.pallas_call(
        prepare_kernel,
        out_shape=(shape((rows, 2 * width + 128), BF), shape((HALF, rows), BF)),
        in_specs=vmem(4),
        out_specs=tuple(vmem(2)),
        cost_estimate=cost(0.1, 2),
        compiler_params=params(8),
    )(tokens, grad_out, gates.T, expert_ids.T)
    spot = jnp.stack([yl, x, c, (z * 2 + yh) * 4]).astype(jnp.int32)
    smem = [pl.BlockSpec(memory_space=pltpu.SMEM)]
    gath = lax.all_gather(pay, "z", axis=0)
    pay_other = shift(pay, "yh", 1)
    n_dev = 2 * n_z
    many = 2 * SLOTS

    p = jnp.arange(n_dev * many)
    dev_p, s_p = p // many, p % many
    q = s_p % SLOTS
    first_of = ((dev_p // 2 * 2 + yh) * 2 + dev_p % 2) * 2
    e_p = first_of + (q >= cap)
    tgt = jnp.where(q < 2 * cap, q % cap + 1, -1)
    sel_s = (e_p[:, None] == jnp.arange(HALF)[None, :]).astype(BF)
    place_s = jnp.broadcast_to(tgt.astype(F32)[:, None], (n_dev * many, 128))
    sent = pl.pallas_call(
        functools.partial(send_kernel, cap),
        out_shape=shape((n_dev, many, width), BF),
        in_specs=vmem(3),
        out_specs=vmem(1)[0],
        cost_estimate=cost(1, 6),
        compiler_params=params(20),
    )(pay_other, sel_s, place_s)
    got_rows = lax.all_to_all(sent, ("z", "c"), 0, 0, tiled=True)

    w_mine = jnp.stack((w_up, jnp.transpose(w_down, (0, 2, 1))), axis=1)
    w_mine = w_mine.reshape(4, share, hidden_len)
    w_mine, _ = held(w_mine, sent)
    w_line = jnp.stack([w_mine] + [shift(w_mine, "yl", d) for d in range(1, n_y)])
    w_parts = [w_line] + [shift(w_line, "x", d) for d in range(1, n_x)]
    gath, *w_parts = held(gath, *w_parts)

    a_own, a_sib = pl.pallas_call(
        functools.partial(pick_kernel, cap),
        out_shape=(shape((2, block, 2 * width + 128), BF),) * 2,
        in_specs=smem + vmem(1),
        out_specs=tuple(vmem(2)),
        cost_estimate=cost(2.6, 12),
        compiler_params=params(20),
    )(spot, gath)
    a_got = shift(a_sib, "c", 1)
    *parts, back = pl.pallas_call(
        functools.partial(expert_kernel, n_y, n_x, cap),
        out_shape=(shape((n_y, 4, share, hidden_len), BF),) * n_x
        + (shape((n_z, 2, 2, many, half), BF),),
        in_specs=smem + vmem(n_x + 3),
        out_specs=tuple(vmem(n_x + 1)),
        scratch_shapes=[
            pltpu.VMEM((4, width, hidden_len), BF),
            pltpu.VMEM((n_y * n_x, 4, share, hidden_len), BF),
            pltpu.VMEM((2, 2, 2 * block, width), BF),
            pltpu.VMEM((4, 2 * block, width), BF),
            pltpu.VMEM((4, 2 * block, 128), BF),
            pltpu.VMEM((3, n_z * many, 2 * block), BF),
        ],
        cost_estimate=cost(9, 24),
        compiler_params=params(44),
    )(spot, *w_parts, a_own, a_got, got_rows.reshape(n_z, 2, many, width))
    got = lax.all_to_all(back.reshape(n_dev, 2, many, half), ("z", "c"), 0, 0, tiled=True)

    lines = [parts[0]] + [shift(parts[d], "x", d) for d in range(1, n_x)]
    line = sum(u.astype(F32) for u in lines).astype(BF)
    ends = [line[0]] + [shift(line[d], "yl", d) for d in range(1, n_y)]
    got, *ends = held(got, *ends)
    grad_up, grad_down = pl.pallas_call(
        total_kernel,
        out_shape=(shape((2, share, hidden_len), BF),) * 2,
        in_specs=vmem(n_y),
        out_specs=tuple(vmem(2)),
        cost_estimate=cost(0, 2),
        compiler_params=params(6),
    )(*ends)
    grad_down = jnp.transpose(grad_down, (0, 2, 1))

    sel_p = (jnp.arange(HALF)[:, None] == e_p[None, :]).astype(BF)
    place_l = jnp.where(s_p < SLOTS, tgt, -1).astype(F32)[None, :]
    place_r = jnp.where(s_p >= SLOTS, tgt, -1).astype(F32)[None, :]
    line_o = jnp.arange(n_dev * 16)
    first_o = ((line_o // 32 * 2 + yh) * 2 + line_o // 16 % 2) * 2
    first_o = jnp.where(line_o % 16 == 2 * cap - 32, first_o, -2)
    parity = jnp.arange(2)[:, None, None]
    owners = (first_o[None, :, None] + parity == jnp.arange(128)[None, None, :]).astype(BF)
    at_slot = jnp.arange(24)[None, :, None]
    slots = (
        (at_slot < cap) & (jnp.arange(128)[None, None, :] == at_slot + parity * cap)
    ).astype(BF)
    partner = pl.pallas_call(
        functools.partial(partner_kernel, cap),
        out_shape=shape((rows, width + 128), BF),
        in_specs=vmem(7),
        out_specs=vmem(1)[0],
        cost_estimate=cost(0.4, 4),
        compiler_params=params(12),
    )(got, pay_other, sel_p, owners, slots, place_l, place_r)
    other = shift(partner, "yh", 1)
    grad_tokens, grad_gates = pl.pallas_call(
        functools.partial(combine_kernel, cap),
        out_shape=(shape((rows, width), BF), shape((top, rows), BF)),
        in_specs=vmem(9),
        out_specs=tuple(vmem(2)),
        cost_estimate=cost(0.4, 4),
        compiler_params=params(12),
    )(got, table, expert_ids.T, sel_p, owners, slots, place_l, place_r, other)
    return (grad_tokens, grad_gates.T, grad_up, grad_down)


def build(mesh):
    every, dp, ctx = ("yl", "x", "z", "yh", "c"), ("yl", "x"), ("z", "yh", "c")
    tok, up, down = P(every, None), P(ctx, dp, None), P(ctx, None, dp)
    return jax.shard_map(
        per_device,
        mesh=mesh,
        in_specs=(tok, tok, tok, tok, up, down),
        out_specs=(tok, tok, up, down),
        check_vma=False,
    )


def solution(mesh):
    return build(Mesh(mesh.devices.reshape(4, 4, 8, 2, 2), ("yl", "x", "z", "yh", "c")))
```
